32 devices in a mesh: seq: 8 (over z, y), chrom: 4 (over x, core).
Axes of the slice: x: 2, y: 2, z: 4, core: 2. Of those that a mesh axis runs over, the one named last changes fastest.
Arguments:
- features: bfloat16 [4, 5120, 768], P('chrom', 'seq'), may hold values from -6 to 6
- first_dilated_taps: bfloat16 [3, 768, 384], replicated, may hold values from -0.125 to 0.125
- first_norm_scale: float32 [384], replicated, may hold values from 0.5 to 2
- first_norm_offset: float32 [384], replicated, may hold values from -3 to 3
- first_pointwise_weight: bfloat16 [384, 768], replicated, may hold values from -0.3125 to 0.3125
- second_dilated_taps: bfloat16 [3, 768, 384], replicated, may hold values from -0.125 to 0.125
- second_norm_scale: float32 [384], replicated, may hold values from 0.5 to 2
- second_norm_offset: float32 [384], replicated, may hold values from -3 to 3
- second_pointwise_weight: bfloat16 [384, 768], replicated, may hold values from -0.3125 to 0.3125
- cotangent: bfloat16 [4, 5120, 768], P('chrom', 'seq'), may hold values from -6 to 6
Outputs:
- grad_input: bfloat16 [4, 5120, 768], P('chrom', 'seq')
- grad_conv_a: float32 [3, 768, 384], P(None, 'seq')
- grad_point_a: float32 [384, 768], P(None, 'seq')
- grad_scale_a: float32 [384], replicated
- grad_shift_a: float32 [384], replicated
- grad_conv_b: float32 [3, 768, 384], P(None, 'seq')
- grad_point_b: float32 [384, 768], P(None, 'seq')
- grad_scale_b: float32 [384], replicated
- grad_shift_b: float32 [384], replicated
The draws below stay inside these ranges and needn't reach their ends.
All inputs are finite; a program needn't handle non-finite values.
Results may differ from the reference program's by a relative error of at most 0.018.
Values may be sent and summed in bfloat16 or wider, within the bound.
No kernel may reach another device: no remote copies, remote signals or barrier semaphores. Data moves between devices by JAX's collectives and lax.ppermute only.
A program may use at most 128 MiB of HBM per device.

```python
import math
import jax
import jax.numpy as jnp
from jax import lax

C = 768
F = 384
DILATION_FIRST = 4096
DILATION_SECOND = 2048
BINS = 5120
CHROMS = 4


def spiked(array, rng, source, target, blocks, factor):
    owner, partner = [(jnp.arange(array.shape[dim]) // (array.shape[dim] // blocks)).reshape([-1 if axis == dim else 1 for axis in range(array.ndim)]) for dim in (source, target)]
    chosen = jax.random.permutation(rng, blocks)[partner]
    strong = (owner == chosen) | (owner == (partner + blocks // 2) % blocks)
    return jnp.where(strong, factor * array, array)


def levels(own_key, shape, split, low, top_value):
    level, own = 1.0, jax.random.fold_in(own_key, 6)
    for axis_at, shards_of in split:
        heights = jnp.exp(jax.random.uniform(jax.random.fold_in(own, axis_at), (shards_of,), jnp.float32, low / len(split), top_value / len(split)))
        level = level * jnp.repeat(heights, shape[axis_at] // shards_of).reshape([-1 if axis == axis_at else 1 for axis in range(len(shape))])
    return level


def centred(key, dims, width, reach, split=(), held_as=jnp.bfloat16):
    drawn = jax.random.normal(key, dims, jnp.float32) * width
    if len(split) > 0:
        drawn = levels(key, dims, split, -0.22, 0.18) * drawn
    return jnp.clip(drawn, min=-reach, max=reach).astype(held_as)


def bell_draw_with(own_key, extent, spread, most, cuts, heavy, held_as=jnp.bfloat16):
    result = spread * jax.random.normal(own_key, extent, jnp.float32)
    if cuts:
        result = result * levels(own_key, extent, cuts, -0.22, 0.18)
    return jnp.clip(spiked(result, jax.random.fold_in(own_key, 3), *heavy), -most, most).astype(held_as)


def setup_inputs(seed: int = 0) -> dict:
    seeds = jax.random.split(jax.random.key(seed), 11)
    features = centred(seeds[0], (CHROMS, BINS, C), 1.0, 6.0, ((0, 4), (1, 8)))
    first_dilated_taps = centred(seeds[1], (3, C, F), (3 * C) ** -0.5, 0.125)
    first_norm_scale = jnp.clip(jnp.exp(jax.random.uniform(seeds[2], (F,), jnp.float32, math.log(0.5), math.log(2.0))), 0.5, 2.0)
    first_norm_offset = centred(seeds[3], (F,), 0.5, 3.0, (), jnp.float32)
    first_pointwise_weight = centred(seeds[4], (F, C), F ** -0.5, 0.3125)
    second_dilated_taps = centred(seeds[5], (3, C, F), (3 * C) ** -0.5, 0.125)
    second_norm_scale = jnp.clip(jnp.exp(jax.random.uniform(seeds[6], (F,), jnp.float32, math.log(0.5), math.log(2.0))), 0.5, 2.0)
    second_norm_offset = centred(seeds[7], (F,), 0.5, 3.0, (), jnp.float32)
    second_pointwise_weight = centred(seeds[8], (F, C), F ** -0.5, 0.3125)
    cotangent = bell_draw_with(seeds[9], (CHROMS, BINS, C), 1.0, 6.0, ((0, 4), (1, 8)), (1, 2, 8, 2.0))
    return {"features": features, "first_dilated_taps": first_dilated_taps, "first_norm_scale": first_norm_scale, "first_norm_offset": first_norm_offset, "first_pointwise_weight": first_pointwise_weight, "second_dilated_taps": second_dilated_taps, "second_norm_scale": second_norm_scale, "second_norm_offset": second_norm_offset, "second_pointwise_weight": second_pointwise_weight, "cotangent": cotangent}


def smooth_value(normed):
    return normed * jax.nn.sigmoid(1.702 * normed)

def smooth_slope(normed):
    sigmoid_part = jax.nn.sigmoid(1.702 * normed)
    return sigmoid_part * (1.0 + 1.702 * normed * (1.0 - sigmoid_part))

def displaced(field, offset):
    rows_all = field.shape[0]
    zero_rows = jnp.zeros((abs(offset), field.shape[1]), field.dtype)
    if offset > 0:
        return jnp.concatenate([field[offset:], zero_rows], 0)
    return jnp.concatenate([zero_rows, field[:rows_all + offset]], 0)

def bottleneck_block_ahead(inputs, conv_weight, bn_scale, bn_shift, dilation):
    before = displaced(inputs, -dilation)
    after = displaced(inputs, dilation)
    pre_act = jnp.dot(before, conv_weight[0], preferred_element_type=jnp.float32)
    pre_act = pre_act + jnp.dot(inputs, conv_weight[1], preferred_element_type=jnp.float32)
    pre_act = pre_act + jnp.dot(after, conv_weight[2], preferred_element_type=jnp.float32)
    normed = bn_scale * pre_act + bn_shift
    activated = smooth_value(normed).astype(jnp.bfloat16)
    return (before, after, pre_act, normed, activated)

def bottleneck_block_reverse(inputs, saved, conv_weight, bn_scale, point_weight, upstream, dilation):
    before, after, pre_act, normed, activated = saved
    grad_act = jnp.dot(upstream, point_weight.T, preferred_element_type=jnp.float32)
    grad_norm = grad_act * smooth_slope(normed)
    grad_pre = (grad_norm * bn_scale).astype(jnp.bfloat16)
    grad_point = jnp.dot(activated.T, upstream, preferred_element_type=jnp.float32)
    grad_scale = lax.optimization_barrier(jnp.sum(grad_norm * pre_act, 0))
    grad_shift = lax.optimization_barrier(jnp.sum(grad_norm, 0))
    grad_conv = jnp.stack([jnp.dot(before.T, grad_pre, preferred_element_type=jnp.float32), jnp.dot(inputs.T, grad_pre, preferred_element_type=jnp.float32), jnp.dot(after.T, grad_pre, preferred_element_type=jnp.float32)])
    grad_in = upstream.astype(jnp.float32) + jnp.dot(grad_pre, conv_weight[1].T, preferred_element_type=jnp.float32)
    grad_in = grad_in + displaced(jnp.dot(grad_pre, conv_weight[0].T, preferred_element_type=jnp.float32), dilation)
    grad_in = grad_in + displaced(jnp.dot(grad_pre, conv_weight[2].T, preferred_element_type=jnp.float32), -dilation)
    return (grad_in.astype(jnp.bfloat16), (grad_conv, grad_point, grad_scale, grad_shift))

def reference(features, first_dilated_taps, first_norm_scale, first_norm_offset, first_pointwise_weight, second_dilated_taps, second_norm_scale, second_norm_offset, second_pointwise_weight, cotangent):
    inputs_out = []
    totals_a = None
    totals_b = None
    for chromosome_index in range(CHROMS):
        first_block_output = features[chromosome_index]
        first_block_stash = bottleneck_block_ahead(first_block_output, first_dilated_taps, first_norm_scale, first_norm_offset, DILATION_FIRST)
        second_block_output = (first_block_output.astype(jnp.float32) + jnp.dot(first_block_stash[4], first_pointwise_weight, preferred_element_type=jnp.float32)).astype(jnp.bfloat16)
        second_block_stash = bottleneck_block_ahead(second_block_output, second_dilated_taps, second_norm_scale, second_norm_offset, DILATION_SECOND)
        second_block_gradient, second_block_partials = bottleneck_block_reverse(second_block_output, second_block_stash, second_dilated_taps, second_norm_scale, second_pointwise_weight, cotangent[chromosome_index], DILATION_SECOND)
        first_block_gradient, first_block_partials = bottleneck_block_reverse(first_block_output, first_block_stash, first_dilated_taps, first_norm_scale, first_pointwise_weight, second_block_gradient, DILATION_FIRST)
        inputs_out.append(first_block_gradient)
        if totals_a is None:
            totals_a, totals_b = (first_block_partials, second_block_partials)
        else:
            totals_a = jax.tree.map(jnp.add, totals_a, first_block_partials)
            totals_b = jax.tree.map(jnp.add, totals_b, second_block_partials)
    factor = 1.0 / math.sqrt(CHROMS * BINS)
    totals_a = [item * factor for item in totals_a]
    totals_b = [item * factor for item in totals_b]
    return (jnp.stack(inputs_out), totals_a[0], totals_a[1], totals_a[2], totals_a[3], totals_b[0], totals_b[1], totals_b[2], totals_b[3])
```

```python
import math

import jax
import jax.numpy as jnp
from jax import lax
from jax.sharding import PartitionSpec as P

DILATION_FIRST = 4096
DILATION_SECOND = 2048
NORM_ROWS = 16


def smooth_value(normed):
    return normed * jax.nn.sigmoid(1.702 * normed)


def smooth_slope(normed):
    sigmoid_part = jax.nn.sigmoid(1.702 * normed)
    return sigmoid_part * (1.0 + 1.702 * normed * (1.0 - sigmoid_part))


def dot(left, right):
    return jnp.dot(left, right, preferred_element_type=jnp.float32)


def to_classes(field, group):
    count = lax.axis_size("seq")
    rows, width = field.shape
    pieces = field.reshape(rows // group, count, group // count, width).transpose(1, 0, 2, 3)
    return lax.all_to_all(pieces, "seq", 0, 0).reshape(rows, width)


def from_classes(field, group):
    count = lax.axis_size("seq")
    rows, width = field.shape
    pieces = field.reshape(count, rows // group, group // count, width)
    pieces = lax.all_to_all(pieces, "seq", 0, 0)
    return pieces.transpose(1, 0, 2, 3).reshape(rows, width)


def add_displaced(middle, from_before, from_after, shift):
    blank = jnp.zeros((shift, middle.shape[1]), middle.dtype)
    middle = middle + jnp.concatenate([blank, from_before], 0)
    return middle + jnp.concatenate([from_after, blank], 0)


def block_ahead(inputs, taps, scale, offset, shift):
    pre = add_displaced(
        dot(inputs, taps[1]), dot(inputs[:-shift], taps[0]), dot(inputs[shift:], taps[2]), shift
    )
    normed = scale * pre + offset
    return pre, normed, smooth_value(normed).astype(jnp.bfloat16)


def block_reverse(inputs, saved, taps, scale, point, upstream, shift):
    pre, normed, activated = saved
    grad_norm = dot(upstream, point.T) * smooth_slope(normed)
    grad_pre = (grad_norm * scale).astype(jnp.bfloat16)
    grads = jnp.stack(
        [
            dot(inputs[:-shift].T, grad_pre[shift:]),
            dot(inputs.T, grad_pre),
            dot(inputs[shift:].T, grad_pre[:-shift]),
            dot(upstream.T, activated),
        ]
    )
    norms = jnp.stack([jnp.sum(grad_norm * pre, 0), jnp.sum(grad_norm, 0)])
    grad_in = add_displaced(
        upstream.astype(jnp.float32) + dot(grad_pre, taps[1].T),
        dot(grad_pre[:-shift], taps[2].T),
        dot(grad_pre[shift:], taps[0].T),
        shift,
    )
    return grad_in.astype(jnp.bfloat16), grads, norms


def split_norms(norms):
    high = lax.reduce_precision(norms, 8, 7)
    parts = jnp.concatenate([high, norms - high], 0).astype(jnp.bfloat16)
    blank = jnp.zeros((NORM_ROWS - parts.shape[0], parts.shape[1]), jnp.bfloat16)
    return jnp.concatenate([parts, blank], 0)


def join_norms(rows):
    rows = rows.astype(jnp.float32)
    return rows[..., 0:2, :] + rows[..., 2:4, :]


def partners(axis, bit):
    return [(i, i ^ bit) for i in range(lax.axis_size(axis))]


def halve(grads, norms, where, axis, bit):
    width = grads.shape[-1]
    kept = lax.dynamic_index_in_dim(grads, where, 0, False)
    sent = lax.dynamic_index_in_dim(grads, 1 - where, 0, False)
    packed = jnp.concatenate([sent.reshape(-1, width), split_norms(norms)], 0)
    came = lax.ppermute(packed, axis, partners(axis, bit))
    other = came[:-NORM_ROWS].reshape(kept.shape)
    total = kept.astype(jnp.float32) + other.astype(jnp.float32)
    return total.astype(jnp.bfloat16), norms + join_norms(came[-NORM_ROWS:])


def settle(grads, norms, seq_first, factor):
    count = lax.axis_size("seq")
    chrom = lax.axis_index("chrom")
    core, across = chrom % 2, chrom // 2
    odd = lax.axis_index("seq") % 2
    kinds, channels, width = grads.shape
    share = channels // count
    grads = grads.astype(jnp.bfloat16).reshape(2, 2, count // 2, 2, share, width)
    grads, norms = halve(grads, norms, core, "chrom", 1)
    if seq_first:
        grads, norms = halve(jnp.moveaxis(grads, 2, 0), norms, odd, "seq", 1)
        grads, norms = halve(grads, norms, across, "chrom", 2)
    else:
        grads, norms = halve(grads, norms, across, "chrom", 2)
        grads, norms = halve(jnp.moveaxis(grads, 1, 0), norms, odd, "seq", 1)
    extra = jnp.broadcast_to(split_norms(norms)[None], (count // 2, NORM_ROWS, width))
    packed = jnp.concatenate([grads, extra], 1)
    groups = [[i for i in range(count) if i % 2 == parity] for parity in range(2)]
    came = lax.all_to_all(packed, "seq", 0, 0, axis_index_groups=groups)
    norms = jnp.sum(join_norms(came[:, share:]), 0)
    mine = jnp.sum(came[:, :share].astype(jnp.float32), 0).astype(jnp.bfloat16)
    other = lax.ppermute(mine, "chrom", partners("chrom", 2))
    pair = jnp.where(across == 0, jnp.stack([mine, other]), jnp.stack([other, mine]))
    other = lax.ppermute(pair, "chrom", partners("chrom", 1))
    full = jnp.where(core == 0, jnp.stack([pair, other]), jnp.stack([other, pair]))
    full = full.reshape(kinds, share, width).astype(jnp.float32) * factor
    norms = norms * factor
    return full[:3], full[3].T, norms[0], norms[1]


def body(
    features,
    first_dilated_taps,
    first_norm_scale,
    first_norm_offset,
    first_pointwise_weight,
    second_dilated_taps,
    second_norm_scale,
    second_norm_offset,
    second_pointwise_weight,
    cotangent,
):
    count = lax.axis_size("seq")
    rows = features.shape[1]
    factor = 1.0 / math.sqrt(rows * count * lax.axis_size("chrom"))
    group = math.gcd(rows, DILATION_SECOND)
    shift_first, shift_second = DILATION_FIRST // count, DILATION_SECOND // count

    inputs = to_classes(features[0], group)
    upstream = to_classes(cotangent[0], group)
    first = block_ahead(
        inputs, first_dilated_taps, first_norm_scale, first_norm_offset, shift_first
    )
    second_inputs = (inputs.astype(jnp.float32) + dot(first[2], first_pointwise_weight)).astype(
        jnp.bfloat16
    )
    second = block_ahead(
        second_inputs, second_dilated_taps, second_norm_scale, second_norm_offset, shift_second
    )
    upstream, grads_b, norms_b = block_reverse(
        second_inputs,
        second,
        second_dilated_taps,
        second_norm_scale,
        second_pointwise_weight,
        upstream,
        shift_second,
    )
    grad_input, grads_a, norms_a = block_reverse(
        inputs,
        first,
        first_dilated_taps,
        first_norm_scale,
        first_pointwise_weight,
        upstream,
        shift_first,
    )
    out_b = settle(grads_b, norms_b, False, factor)
    out_a = settle(grads_a, norms_a, True, factor)
    return (from_classes(grad_input, group)[None], *out_a, *out_b)


def solution(mesh):
    in_specs = (
        P("chrom", "seq", None),
        P(),
        P(),
        P(),
        P(),
        P(),
        P(),
        P(),
        P(),
        P("chrom", "seq", None),
    )
    out_specs = (
        P("chrom", "seq", None),
        P(None, "seq", None),
        P(None, "seq"),
        P(),
        P(),
        P(None, "seq", None),
        P(None, "seq"),
        P(),
        P(),
    )
    return jax.shard_map(body, mesh=mesh, in_specs=in_specs, out_specs=out_specs, check_vma=False)
```

```python
import functools
import math

import jax
import jax.numpy as jnp
from jax import lax
from jax.experimental import pallas as pl
from jax.experimental.pallas import tpu as pltpu
from jax.sharding import PartitionSpec as P

DILATION_FIRST = 4096
DILATION_SECOND = 2048
NORM_ROWS = 16
VMEM_BYTES = 56 * 2**20
LATER_VMEM_BYTES = 24 * 2**20

IN_VMEM = pl.BlockSpec(memory_space=pltpu.VMEM)
ANYWHERE = pl.BlockSpec(memory_space=pl.ANY)


def smooth_value(normed):
    return normed * jax.nn.sigmoid(1.702 * normed)


def smooth_slope(normed):
    sigmoid_part = jax.nn.sigmoid(1.702 * normed)
    return sigmoid_part * (1.0 + 1.702 * normed * (1.0 - sigmoid_part))


def dot(left, right):
    return jnp.dot(left, right, preferred_element_type=jnp.float32)


def across(left, right):
    return lax.dot_general(left, right, (((1,), (1,)), ((), ())), preferred_element_type=jnp.float32)


def over_rows(left, right):
    return lax.dot_general(left, right, (((0,), (0,)), ((), ())), preferred_element_type=jnp.float32)


def pick(values, index):
    chosen = jnp.int32(int(values[0]))
    for at, value in enumerate(values[1:], 1):
        chosen = jnp.where(index == at, jnp.int32(int(value)), chosen)
    return chosen


class Routes:
    def __init__(self, rows, count):
        self.unit = math.gcd(rows, DILATION_SECOND // count)
        self.units = rows // self.unit
        same = math.gcd(self.units, count)
        permutes = []
        for j in range(self.units):
            permute = {}
            for i in range(count):
                slot = j // same * same + (j + i // (count // same)) % same
                whole = self.units * i + slot
                permute[i] = slot, whole % count, whole // count
            permutes.append(permute)
        stay, moved = self.without_stays(permutes, count)
        self.stay = stay
        self.permutes = permutes if stay is None else moved
        for permute in self.permutes:
            assert len({target for _, target, _ in permute.values()}) == count

    @staticmethod
    def without_stays(permutes, count):
        stay, moved = {}, []
        for permute in permutes:
            rest = {}
            for i, (slot, target, place) in permute.items():
                if target == i and i not in stay:
                    stay[i] = slot, place
                else:
                    rest[i] = slot, target, place
            for other in moved:
                targets = {target for _, target, _ in other.values()}
                if not (other.keys() & rest.keys()) and not any(t in targets for _, t, _ in rest.values()):
                    other.update(rest)
                    break
            else:
                moved.append(rest)
        if len(stay) != count or any(len(permute) != count for permute in moved):
            return None, None
        return stay, moved

    def slots(self):
        count = len(self.permutes[0])
        found = [[permute[i][0] for i in range(count)] for permute in self.permutes]
        return found if self.stay is None else found + [[self.stay[i][0] for i in range(count)]]

    def places(self):
        count = len(self.permutes[0])
        found = []
        for permute in self.permutes:
            by_target = {target: place for _, target, place in permute.values()}
            found.append([by_target[k] for k in range(count)])
        return found if self.stay is None else found + [[self.stay[k][1] for k in range(count)]]

    def out(self, field):
        mine = lax.axis_index("seq")
        came = []
        for permute in self.permutes:
            slots = [permute[i][0] for i in range(len(permute))]
            if len(set(slots)) == 1:
                part = field[slots[0] * self.unit : (slots[0] + 1) * self.unit]
            else:
                part = lax.dynamic_slice_in_dim(field, jnp.asarray(slots)[mine] * self.unit, self.unit, 0)
            came.append(lax.ppermute(part, "seq", [(i, t) for i, (_, t, _) in permute.items()]))
        return came

    def back(self, parts):
        return [
            lax.ppermute(part, "seq", [(t, i) for i, (_, t, _) in permute.items()])
            for part, permute in zip(parts, self.permutes)
        ]


def fetch(source, target, sem):
    copy = pltpu.make_async_copy(source, target, sem)
    copy.start()
    return copy


def unit_at(ref, place, unit):
    return ref.at[pl.ds(pl.multiple_of(place * unit, unit), unit), :]


def fetch_units(routes, field, came, target, sems, first):
    mine = lax.axis_index("seq")
    places, slots, unit = routes.places(), routes.slots(), routes.unit
    copies = []
    for j, place in enumerate(places):
        source = came[j] if j < len(came) else unit_at(field, pick(slots[j], mine), unit)
        copies.append(fetch(source, unit_at(target, pick(place, mine), unit), sems.at[first + j]))
    return copies


def wait_all(copies):
    for copy in copies:
        copy.wait()


def padded(share):
    return -(-share // 16) * 16


def row_parts(rows):
    step = math.gcd(rows, 128)
    return rows // step, step


def ahead_kernel(routes, shifts, *refs):
    steps, units = len(routes.permutes), routes.units
    field, slots, refs = refs[0], refs[1 : 1 + steps], refs[1 + steps :]
    taps_hbm, point_hbm, taps_b_hbm = refs[:3]
    scale_a, offset_a, scale_b, offset_b = refs[3:7]
    outs, refs = refs[7:12], refs[12:]
    inputs, taps, point, taps_b, pre_a, act_a, second, pre_b, act_b, sems = refs
    rows, width = pre_a.shape
    load_taps = fetch(taps_hbm, taps, sems.at[units])
    came = fetch_units(routes, field, slots, inputs, sems, 0)
    load_point = fetch(point_hbm, point, sems.at[units + 1])
    load_taps_b = fetch(taps_b_hbm, taps_b, sems.at[units + 2])

    def block(field, taps, scale_ref, offset_ref, pre, act, shift):
        pre[...] = dot(field[...], taps[1])
        pre[shift:, :] += dot(field[:-shift, :], taps[0])
        pre[:-shift, :] += dot(field[shift:, :], taps[2])
        scale, offset = scale_ref[...][None, :], offset_ref[...][None, :]
        steps, step = row_parts(rows)

        @pl.loop(0, steps)
        def _(at):
            part = pl.ds(pl.multiple_of(at * step, step), step)
            act[part, :] = smooth_value(scale * pre[part, :] + offset).astype(jnp.bfloat16)

    def leave(index, source):
        return fetch(source, outs[index], sems.at[units + 3 + index])

    wait_all(came)
    load_taps.wait()
    block(inputs, taps, scale_a, offset_a, pre_a, act_a, shifts[0])
    left = [leave(0, pre_a), leave(1, act_a)]
    load_point.wait()
    second[...] = (inputs[...].astype(jnp.float32) + dot(act_a[...], point[...])).astype(jnp.bfloat16)
    left += [leave(2, second)]
    load_taps_b.wait()
    block(second, taps_b, scale_b, offset_b, pre_b, act_b, shifts[1])
    wait_all(left + [leave(3, pre_b), leave(4, act_b)])


def ahead(routes, field, slots, first, second, shifts, rows):
    (taps, scale_a, offset_a, point), (taps_b, scale_b, offset_b, _) = first, second
    channels, width = taps.shape[1:]
    units = routes.units
    shape = jax.ShapeDtypeStruct
    thin, wide = (rows, width), (rows, channels)
    return pl.pallas_call(
        functools.partial(ahead_kernel, routes, shifts),
        out_shape=(
            shape(thin, jnp.float32),
            shape(thin, jnp.bfloat16),
            shape(wide, jnp.bfloat16),
            shape(thin, jnp.float32),
            shape(thin, jnp.bfloat16),
        ),
        in_specs=[ANYWHERE] * (1 + len(slots) + 3) + [IN_VMEM] * 4,
        out_specs=[ANYWHERE] * 5,
        scratch_shapes=[
            pltpu.VMEM(wide, jnp.bfloat16),
            pltpu.VMEM(taps.shape, jnp.bfloat16),
            pltpu.VMEM(point.shape, jnp.bfloat16),
            pltpu.VMEM(taps.shape, jnp.bfloat16),
            pltpu.VMEM(thin, jnp.float32),
            pltpu.VMEM(thin, jnp.bfloat16),
            pltpu.VMEM(wide, jnp.bfloat16),
            pltpu.VMEM(thin, jnp.float32),
            pltpu.VMEM(thin, jnp.bfloat16),
            pltpu.SemaphoreType.DMA((units + 8,)),
        ],
        compiler_params=pltpu.CompilerParams(vmem_limit_bytes=VMEM_BYTES),
        cost_estimate=pl.CostEstimate(
            flops=2 * width * channels * 5 * rows,
            bytes_accessed=10 * 2**20,
            transcendentals=2 * rows * width,
        ),
    )(field, *slots, taps, point, taps_b, scale_a, offset_a, scale_b, offset_b)


def split_norms(norms):
    high = norms.astype(jnp.bfloat16)
    low = (norms - high.astype(jnp.float32)).astype(jnp.bfloat16)
    blank = jnp.zeros((NORM_ROWS - 2 * norms.shape[0], norms.shape[1]), jnp.bfloat16)
    return jnp.concatenate([high, low, blank], 0)


def join_norms(rows, count):
    rows = rows.astype(jnp.float32)
    return rows[:count] + rows[count : 2 * count]


def reverse_kernel(routes, count, shifts, *refs):
    steps, units, unit = len(routes.permutes), routes.units, routes.unit
    u_field, u_slots, refs = refs[0], refs[1 : 1 + steps], refs[1 + steps :]
    g_field, g_slots, refs = refs[0], refs[1 : 1 + steps], refs[1 + steps :]
    second_hbm, pre_b_hbm, act_b_hbm, pre_a_hbm, act_a_hbm = refs[:5]
    taps_b_hbm, point_b_hbm, taps_a_hbm, point_a_hbm = refs[5:9]
    scale_a, offset_a, scale_b, offset_b = refs[9:13]
    places = routes.places()
    grad_slots, refs = refs[13 : 13 + len(places)], refs[13 + len(places) :]
    kept_b, sent_b, kept_a, sent_a, norms_ref = refs[:5]
    u_a, g_a, u_b, g_b, pre_a, pre_b, act_a, act_b, taps_a, taps_b, point_a, point_b = refs[5:17]
    grad_act, grad_pre, product, staged, wide, sums, norm_rows, sems, out_sems = refs[17:]
    rows, width = pre_a.shape
    channels = u_a.shape[1]
    share = channels // count
    pad = padded(share)
    half = count // 2 * pad
    seq, chrom = lax.axis_index("seq"), lax.axis_index("chrom")
    core, side, odd, rest = chrom % 2, chrom // 2, seq % 2, seq // 2

    def load(at, source, target):
        return fetch(source, target, sems.at[2 * units + at])

    came_g = fetch_units(routes, g_field, g_slots, g_b, sems, 0)
    loads_b = [load(0, point_b_hbm, point_b), load(1, pre_b_hbm, pre_b)]
    came_second = [load(2, second_hbm, u_b)]
    loads_b += [load(3, act_b_hbm, act_b), load(4, taps_b_hbm, taps_b)]
    loads_a = [load(5, point_a_hbm, point_a), load(6, pre_a_hbm, pre_a)]
    came_u = fetch_units(routes, u_field, u_slots, u_a, sems, units)
    loads_a += [load(7, act_a_hbm, act_a), load(8, taps_a_hbm, taps_a)]

    def block(index, u, g, pre, act, taps, point, loads, came, scale_ref, offset_ref, shift, kept, sent):
        scale, offset = scale_ref[...][None, :], offset_ref[...][None, :]
        loads[0].wait()
        grad_act[...] = across(g[...], point[...])
        sums[...] = jnp.zeros_like(sums)
        steps, step = row_parts(rows)
        loads[1].wait()

        @pl.loop(0, steps)
        def _(at):
            part = pl.ds(pl.multiple_of(at * step, step), step)
            value = pre[part, :]
            normed = scale * value + offset
            grad_norm = grad_act[part, :] * smooth_slope(normed)
            grad_pre[part, :] = (grad_norm * scale).astype(jnp.bfloat16)
            sums[0] += jnp.sum((grad_norm * value).reshape(step // 8, 8, width), 0)
            sums[1] += jnp.sum(grad_norm.reshape(step // 8, 8, width), 0)

        norms = jnp.sum(sums[...], 1)
        norms_ref[2 * index : 2 * index + 2, :] = norms
        norm_rows[index] = split_norms(norms)
        tail = fetch(norm_rows.at[index], sent.at[pl.ds(4 * half, NORM_ROWS)], out_sems.at[index, 8])

        def copies(kind, target):
            source = staged.at[4 * index + kind]
            slot = (kind % 2) ^ side
            for part in range(2):
                place = (slot * 2 + part if index == 1 else part * 2 + slot) * half
                yield pltpu.make_async_copy(
                    source.at[pl.ds(part * half, half)],
                    target.at[pl.ds(pl.multiple_of(place, half), half)],
                    out_sems.at[index, 2 * kind + part],
                )

        def both(kind, act_on):
            @pl.when(core == kind // 2)
            def _():
                for copy in copies(kind, kept):
                    act_on(copy)

            @pl.when(core != kind // 2)
            def _():
                for copy in copies(kind, sent):
                    act_on(copy)

        def settle_one(kind, value):
            product[:channels, :] = value
            for at in range(count):
                place = ((at % 2) ^ odd) * half + ((at // 2) ^ rest) * pad
                staged[4 * index + kind, pl.ds(pl.multiple_of(place, pad), pad), :] = product[
                    at * share : at * share + pad, :
                ].astype(jnp.bfloat16)
            both(kind, lambda copy: copy.start())

        wait_all(came)
        settle_one(0, over_rows(u[:-shift, :], grad_pre[shift:, :]))
        settle_one(1, over_rows(u[...], grad_pre[...]))
        settle_one(2, over_rows(u[shift:, :], grad_pre[:-shift, :]))
        loads[2].wait()
        settle_one(3, over_rows(g[...], act[...]))
        loads[3].wait()
        wide[...] = across(grad_pre[...], taps[1])
        wide[:-shift, :] += across(grad_pre[shift:, :], taps[0])
        wide[shift:, :] += across(grad_pre[:-shift, :], taps[2])
        g_a[...] = (wide[...] + g[...].astype(jnp.float32)).astype(jnp.bfloat16)

        def finish():
            tail.wait()
            for kind in range(4):
                both(kind, lambda copy: copy.wait())

        return finish

    wait_all(came_g)
    finish_b = block(
        1, u_b, g_b, pre_b, act_b, taps_b, point_b, loads_b, came_second, scale_b, offset_b, shifts[1], kept_b, sent_b
    )
    finish_a = block(
        0, u_a, g_a, pre_a, act_a, taps_a, point_a, loads_a, came_u, scale_a, offset_a, shifts[0], kept_a, sent_a
    )
    grads = [
        fetch(unit_at(g_a, pick(places[j], seq), unit), slot, sems.at[j])
        for j, slot in enumerate(grad_slots)
    ]
    finish_b()
    finish_a()
    wait_all(grads)


def reverse(routes, u_field, u_slots, g_field, g_slots, saved, first, second, shifts, rows):
    (taps_a, scale_a, offset_a, point_a), (taps_b, scale_b, offset_b, point_b) = first, second
    pre_a, act_a, second_inputs, pre_b, act_b = saved
    channels, width = taps_a.shape[1:]
    units, count = routes.units, lax.axis_size("seq")
    went = len(routes.places())
    shape = jax.ShapeDtypeStruct
    thin, wide = (rows, width), (rows, channels)
    pad = padded(channels // count)
    kept = shape((2 * count * pad, width), jnp.bfloat16)
    sent = shape((2 * count * pad + NORM_ROWS, width), jnp.bfloat16)
    vmem = pltpu.VMEM
    outs = pl.pallas_call(
        functools.partial(reverse_kernel, routes, count, shifts),
        out_shape=(
            *[shape((routes.unit, channels), jnp.bfloat16)] * went,
            kept,
            sent,
            kept,
            sent,
            shape((4, width), jnp.float32),
        ),
        in_specs=[ANYWHERE] * (2 + len(u_slots) + len(g_slots) + 9) + [IN_VMEM] * 4,
        out_specs=[ANYWHERE] * (went + 4) + [IN_VMEM],
        scratch_shapes=[
            *[vmem(wide, jnp.bfloat16)] * 4,
            *[vmem(thin, jnp.float32)] * 2,
            *[vmem(thin, jnp.bfloat16)] * 2,
            *[vmem(taps_a.shape, jnp.bfloat16)] * 2,
            *[vmem(point_a.shape, jnp.bfloat16)] * 2,
            vmem(thin, jnp.float32),
            vmem(thin, jnp.bfloat16),
            vmem((channels + pad - channels // count, width), jnp.float32),
            vmem((8, count * pad, width), jnp.bfloat16),
            vmem(wide, jnp.float32),
            vmem((2, 8, width), jnp.float32),
            vmem((2, NORM_ROWS, width), jnp.bfloat16),
            pltpu.SemaphoreType.DMA((2 * units + 9,)),
            pltpu.SemaphoreType.DMA((2, 9)),
        ],
        compiler_params=pltpu.CompilerParams(vmem_limit_bytes=VMEM_BYTES),
        cost_estimate=pl.CostEstimate(
            flops=2 * width * channels * 11 * rows,
            bytes_accessed=18 * 2**20,
            transcendentals=2 * rows * width,
        ),
    )(
        u_field, *u_slots, g_field, *g_slots, second_inputs, pre_b, act_b, pre_a, act_a,
        taps_b, point_b, taps_a, point_a,
        scale_a, offset_a, scale_b, offset_b,
    )
    return outs[:went], outs[went : went + 4], outs[went + 4]


def gather_kernel(routes, *refs):
    parts, out = refs[:-1], refs[-1]
    mine, unit = lax.axis_index("seq"), routes.unit
    for slots, part in zip(routes.slots(), parts):
        out[pl.ds(pl.multiple_of(pick(slots, mine) * unit, unit), unit), :] = part[...]


def gather_units(routes, parts):
    unit, channels = parts[0].shape
    return pl.pallas_call(
        functools.partial(gather_kernel, routes),
        out_shape=jax.ShapeDtypeStruct((routes.units * unit, channels), jnp.bfloat16),
        in_specs=[IN_VMEM] * len(parts),
        out_specs=IN_VMEM,
        cost_estimate=pl.CostEstimate(flops=0, bytes_accessed=2**21, transcendentals=0),
    )(*parts)


def trade(value, axis, bits):
    return lax.ppermute(value, axis, [(i, i ^ bits) for i in range(lax.axis_size(axis))])


def rows_at(block, index, width):
    return pl.BlockSpec((block, width), lambda step: (index, 0))


def summed(parts):
    total = parts[0][...].astype(jnp.float32)
    for part in parts[1:]:
        total = total + part[...].astype(jnp.float32)
    return total


def combine_kernel(number, norms_in, *refs):
    outs = refs[2 * number + 2 : 2 * number + 4]
    norms_out = refs[2 * number + 4]
    for block in range(2):
        parts = refs[block * (number + 1) : (block + 1) * (number + 1)]
        size = parts[0].shape[0]
        norms = norms_in[2 * block : 2 * block + 2, :] + join_norms(parts[number][...], 2)
        norms_out[2 * block : 2 * block + 2, :] = norms
        outs[block][:size, :] = summed(parts[:number]).astype(jnp.bfloat16)
        outs[block][size:, :] = split_norms(norms)


def combine(norms, parts_a, parts_b, waited, vmem_bytes):
    number, width = len(parts_a), norms.shape[1]
    size = (parts_a[-1].shape[0] - NORM_ROWS) // 2
    specs = [rows_at(size, 1, width)] * number + [rows_at(NORM_ROWS, 2 * size // NORM_ROWS, width)]
    shape = jax.ShapeDtypeStruct
    payload = shape((size + NORM_ROWS, width), jnp.bfloat16)
    whole = pl.BlockSpec(payload.shape, lambda step: (0, 0))
    small = pl.BlockSpec(norms.shape, lambda step: (0, 0))

    def kernel(*refs):
        combine_kernel(number, refs[0], *refs[1 : 2 * number + 3], *refs[2 * number + 3 + len(waited) :])

    return pl.pallas_call(
        kernel,
        grid=(1,),
        out_shape=(payload, payload, shape(norms.shape, jnp.float32)),
        in_specs=[small] + specs * 2 + [ANYWHERE] * len(waited),
        out_specs=(whole, whole, small),
        compiler_params=pltpu.CompilerParams(vmem_limit_bytes=vmem_bytes),
        cost_estimate=pl.CostEstimate(flops=0, bytes_accessed=8 * size * width * number, transcendentals=0),
    )(norms, *parts_a, parts_a[-1], *parts_b, parts_b[-1], *waited)


def pieces_kernel(number, norms_in, *refs):
    parts, refs = refs[: 2 * number + 2], refs[2 * number + 2 :]
    mine, norms_out, payloads, total = refs[0], refs[1], refs[2:-1], refs[-1]
    pad = mine.shape[0] // 2
    norms = []
    for block in range(2):
        own = parts[block * (number + 1) : (block + 1) * (number + 1)]
        norms.append(norms_in[2 * block : 2 * block + 2, :] + join_norms(own[number][...], 2))
        total[...] = summed(own[:number])
        mine[block * pad : (block + 1) * pad, :] = total[:pad, :]
        for at, payload in enumerate(payloads, 1):
            payload[block * pad : (block + 1) * pad, :] = total[
                at * pad : (at + 1) * pad, :
            ].astype(jnp.bfloat16)
    norms = jnp.concatenate(norms, 0)
    norms_out[...] = norms
    for payload in payloads:
        payload[2 * pad :, :] = split_norms(norms)


def cut_pieces(norms, parts_a, parts_b, share):
    number, width = len(parts_a), norms.shape[1]
    size = parts_a[-1].shape[0] - NORM_ROWS
    pad = padded(share)
    shape = jax.ShapeDtypeStruct
    specs = [rows_at(size, 0, width)] * number + [rows_at(NORM_ROWS, size // NORM_ROWS, width)]
    outs = (
        shape((2 * pad, width), jnp.float32),
        shape(norms.shape, jnp.float32),
        *[shape((2 * pad + NORM_ROWS, width), jnp.bfloat16)] * (size // pad - 1),
    )
    return pl.pallas_call(
        functools.partial(pieces_kernel, number),
        grid=(1,),
        out_shape=outs,
        in_specs=[pl.BlockSpec(norms.shape, lambda step: (0, 0))] + specs * 2,
        out_specs=[pl.BlockSpec(out.shape, lambda step: (0, 0)) for out in outs],
        scratch_shapes=[pltpu.VMEM((size, width), jnp.float32)],
        compiler_params=pltpu.CompilerParams(vmem_limit_bytes=LATER_VMEM_BYTES),
        cost_estimate=pl.CostEstimate(flops=0, bytes_accessed=8 * size * width * number, transcendentals=0),
    )(norms, *parts_a, parts_a[-1], *parts_b, parts_b[-1])


def total_kernel(norms_in, mine, *refs):
    came, out, norms_out = refs[:-2], refs[-2], refs[-1]
    rows = mine.shape[0]
    total, norms = mine[...], norms_in[...]
    for payload in came:
        total = total + payload[:rows, :].astype(jnp.float32)
        norms = norms + join_norms(payload[rows:, :], norms.shape[0])
    out[...] = total.astype(jnp.bfloat16)
    norms_out[...] = norms


def add_pieces(norms, mine, came):
    return pl.pallas_call(
        total_kernel,
        out_shape=(
            jax.ShapeDtypeStruct(mine.shape, jnp.bfloat16),
            jax.ShapeDtypeStruct(norms.shape, jnp.float32),
        ),
        in_specs=[IN_VMEM] * (2 + len(came)),
        out_specs=[IN_VMEM] * 2,
        compiler_params=pltpu.CompilerParams(vmem_limit_bytes=LATER_VMEM_BYTES),
        cost_estimate=pl.CostEstimate(flops=0, bytes_accessed=2**20, transcendentals=0),
    )(norms, mine, *came)


def finish_kernel(factor, share, norms_in, *refs):
    pieces, outs, norms_out = refs[:4], refs[4:8], refs[8:]
    chrom = lax.axis_index("chrom")
    mine = chrom % 2 * 2 + chrom // 2
    for row, out in enumerate(norms_out):
        out[...] = norms_in[row, :] * factor
    pad = pieces[0].shape[0] // 2
    for block in range(2):
        taps, point = outs[2 * block : 2 * block + 2]
        for bits in range(4):
            kind = mine ^ bits
            value = pieces[bits][block * pad : block * pad + share, :].astype(jnp.float32) * factor

            @pl.when(kind < 3)
            def _():
                taps[jnp.minimum(kind, 2)] = value

            @pl.when(kind == 3)
            def _():
                point[...] = value


def finish(norms, pieces, share, factor):
    width = norms.shape[1]
    shape = jax.ShapeDtypeStruct
    pair = [shape((3, share, width), jnp.float32), shape((share, width), jnp.float32)]
    return pl.pallas_call(
        functools.partial(finish_kernel, factor, share),
        out_shape=(*pair, *pair, *[shape((width,), jnp.float32)] * 4),
        in_specs=[IN_VMEM] * 5,
        out_specs=[IN_VMEM] * 8,
        cost_estimate=pl.CostEstimate(flops=0, bytes_accessed=2 * 2**20, transcendentals=0),
    )(norms, *pieces)


def settle(halves, norms, waited, share, factor):
    kept_b, sent_b, kept_a, sent_a = halves
    parts_b, parts_a = [kept_b, trade(sent_b, "chrom", 1)], [kept_a, trade(sent_a, "chrom", 1)]
    sent_a, sent_b, norms = combine(norms, parts_a, parts_b, waited[3:], VMEM_BYTES)
    parts_b.append(trade(sent_b, "chrom", 2))
    parts_a.append(trade(sent_a, "seq", 1))
    sent_a, sent_b, norms = combine(norms, parts_a, parts_b, waited[:3], LATER_VMEM_BYTES)
    parts_b.append(trade(sent_b, "seq", 1))
    parts_a.append(trade(sent_a, "chrom", 2))
    mine, norms, *payloads = cut_pieces(norms, parts_a, parts_b, share)
    came = [trade(payload, "seq", 2 * b) for b, payload in enumerate(payloads, 1)]
    mine, norms = add_pieces(norms, mine, came)
    pieces = [mine] + [trade(mine, "chrom", bits) for bits in (2, 1, 3)]
    return finish(norms, pieces, share, factor)


def body(
    features,
    first_dilated_taps,
    first_norm_scale,
    first_norm_offset,
    first_pointwise_weight,
    second_dilated_taps,
    second_norm_scale,
    second_norm_offset,
    second_pointwise_weight,
    cotangent,
):
    count = lax.axis_size("seq")
    rows = features.shape[1]
    factor = 1.0 / math.sqrt(rows * count * lax.axis_size("chrom"))
    shifts = DILATION_FIRST // count, DILATION_SECOND // count
    routes = Routes(rows, count)
    first = first_dilated_taps, first_norm_scale, first_norm_offset, first_pointwise_weight
    second = second_dilated_taps, second_norm_scale, second_norm_offset, second_pointwise_weight
    u_slots = routes.out(features[0])
    g_slots = routes.out(cotangent[0])
    saved = ahead(routes, features[0], u_slots, first, second, shifts, rows)
    grads, halves, norms = reverse(
        routes, features[0], u_slots, cotangent[0], g_slots, saved, first, second, shifts, rows
    )
    came = routes.back(grads)
    share = features.shape[2] // count
    conv_a, point_a, conv_b, point_b, *norms = settle(halves, norms, came, share, factor)
    grad_input = gather_units(routes, came + list(grads[len(came) :]))[None]
    return (
        grad_input,
        conv_a, point_a.T, norms[0], norms[1],
        conv_b, point_b.T, norms[2], norms[3],
    )


def solution(mesh):
    in_specs = (
        P("chrom", "seq", None),
        P(),
        P(),
        P(),
        P(),
        P(),
        P(),
        P(),
        P(),
        P("chrom", "seq", None),
    )
    out_specs = (
        P("chrom", "seq", None),
        P(None, "seq", None),
        P(None, "seq"),
        P(),
        P(),
        P(None, "seq", None),
        P(None, "seq"),
        P(),
        P(),
    )
    return jax.shard_map(body, mesh=mesh, in_specs=in_specs, out_specs=out_specs, check_vma=False)
```

```python
import functools
import math

import jax
import jax.numpy as jnp
from jax import lax
from jax.experimental import pallas as pl
from jax.experimental.pallas import tpu as pltpu
from jax.sharding import PartitionSpec as P

DILATION_FIRST = 4096
DILATION_SECOND = 2048
NORM_ROWS = 16
VMEM_BYTES = 56 * 2**20
LATER_VMEM_BYTES = 24 * 2**20

IN_VMEM = pl.BlockSpec(memory_space=pltpu.VMEM)
ANYWHERE = pl.BlockSpec(memory_space=pl.ANY)


def smooth_value(normed):
    return normed * jax.nn.sigmoid(1.702 * normed)


def smooth_slope(normed):
    sigmoid_part = jax.nn.sigmoid(1.702 * normed)
    return sigmoid_part * (1.0 + 1.702 * normed * (1.0 - sigmoid_part))


def dot(left, right):
    return jnp.dot(left, right, preferred_element_type=jnp.float32)


def across(left, right):
    return lax.dot_general(left, right, (((1,), (1,)), ((), ())), preferred_element_type=jnp.float32)


def over_rows(left, right):
    return lax.dot_general(left, right, (((0,), (0,)), ((), ())), preferred_element_type=jnp.float32)


def pick(values, index):
    chosen = jnp.int32(int(values[0]))
    for at, value in enumerate(values[1:], 1):
        chosen = jnp.where(index == at, jnp.int32(int(value)), chosen)
    return chosen


class Routes:
    def __init__(self, rows, count):
        self.unit = math.gcd(rows, DILATION_SECOND // count)
        self.units = rows // self.unit
        same = math.gcd(self.units, count)
        permutes = []
        for j in range(self.units):
            permute = {}
            for i in range(count):
                slot = j // same * same + (j + i // (count // same)) % same
                whole = self.units * i + slot
                permute[i] = slot, whole % count, whole // count
            permutes.append(permute)
        stay, moved = self.without_stays(permutes, count)
        self.stay = stay
        self.permutes = permutes if stay is None else moved
        for permute in self.permutes:
            assert len({target for _, target, _ in permute.values()}) == count

    @staticmethod
    def without_stays(permutes, count):
        stay, moved = {}, []
        for permute in permutes:
            rest = {}
            for i, (slot, target, place) in permute.items():
                if target == i and i not in stay:
                    stay[i] = slot, place
                else:
                    rest[i] = slot, target, place
            for other in moved:
                targets = {target for _, target, _ in other.values()}
                if not (other.keys() & rest.keys()) and not any(t in targets for _, t, _ in rest.values()):
                    other.update(rest)
                    break
            else:
                moved.append(rest)
        if len(stay) != count or any(len(permute) != count for permute in moved):
            return None, None
        return stay, moved

    def slots(self):
        count = len(self.permutes[0])
        found = [[permute[i][0] for i in range(count)] for permute in self.permutes]
        return found if self.stay is None else found + [[self.stay[i][0] for i in range(count)]]

    def places(self):
        count = len(self.permutes[0])
        found = []
        for permute in self.permutes:
            by_target = {target: place for _, target, place in permute.values()}
            found.append([by_target[k] for k in range(count)])
        return found if self.stay is None else found + [[self.stay[k][1] for k in range(count)]]

    def out(self, field):
        mine = lax.axis_index("seq")
        came = []
        for permute in self.permutes:
            slots = [permute[i][0] for i in range(len(permute))]
            kinds = sorted(set(slots))
            part = field[kinds[0] * self.unit : (kinds[0] + 1) * self.unit]
            for kind in kinds[1:]:
                other = field[kind * self.unit : (kind + 1) * self.unit]
                part = jnp.where(pick([slot == kind for slot in slots], mine) == 1, other, part)
            came.append(lax.ppermute(part, "seq", [(i, t) for i, (_, t, _) in permute.items()]))
        return came

    def back(self, parts):
        return [
            lax.ppermute(part, "seq", [(t, i) for i, (_, t, _) in permute.items()])
            for part, permute in zip(parts, self.permutes)
        ]


def fetch(source, target, sem):
    copy = pltpu.make_async_copy(source, target, sem)
    copy.start()
    return copy


def unit_at(ref, place, unit):
    return ref.at[pl.ds(pl.multiple_of(place * unit, unit), unit), :]


def fetch_units(routes, field, came, target, sems, first):
    mine = lax.axis_index("seq")
    places, slots, unit = routes.places(), routes.slots(), routes.unit
    copies = []
    for j, place in enumerate(places):
        source = came[j] if j < len(came) else unit_at(field, pick(slots[j], mine), unit)
        copies.append(fetch(source, unit_at(target, pick(place, mine), unit), sems.at[first + j]))
    return copies


def wait_all(copies):
    for copy in copies:
        copy.wait()


def padded(share):
    return -(-share // 16) * 16


def row_parts(rows):
    step = math.gcd(rows, 32)
    return rows // step, step


def ahead_kernel(routes, shifts, *refs):
    steps, units = len(routes.permutes), routes.units
    field, slots, refs = refs[0], refs[1 : 1 + steps], refs[1 + steps :]
    taps_hbm, point_hbm, taps_b_hbm = refs[:3]
    scale_a, offset_a, scale_b, offset_b = refs[3:7]
    outs, refs = refs[7:12], refs[12:]
    inputs, taps, point, taps_b, pre_a, act_a, second, pre_b, act_b, sems = refs
    rows, width = pre_a.shape
    load_taps = fetch(taps_hbm, taps, sems.at[units])
    came = fetch_units(routes, field, slots, inputs, sems, 0)
    load_point = fetch(point_hbm, point, sems.at[units + 1])
    load_taps_b = fetch(taps_b_hbm, taps_b, sems.at[units + 2])

    def block(field, taps, scale_ref, offset_ref, pre, act, shift):
        pre[...] = dot(field[...], taps[1])
        pre[shift:, :] += dot(field[:-shift, :], taps[0])
        pre[:-shift, :] += dot(field[shift:, :], taps[2])
        scale, offset = scale_ref[...][None, :], offset_ref[...][None, :]
        steps, step = row_parts(rows)

        @pl.loop(0, steps, unroll=2 if steps % 2 == 0 else 1)
        def _(at):
            part = pl.ds(pl.multiple_of(at * step, step), step)
            act[part, :] = smooth_value(scale * pre[part, :] + offset).astype(jnp.bfloat16)

    def leave(index, source):
        return fetch(source, outs[index], sems.at[units + 3 + index])

    wait_all(came)
    load_taps.wait()
    block(inputs, taps, scale_a, offset_a, pre_a, act_a, shifts[0])
    left = [leave(0, pre_a), leave(1, act_a)]
    load_point.wait()
    second[...] = (inputs[...].astype(jnp.float32) + dot(act_a[...], point[...])).astype(jnp.bfloat16)
    left += [leave(2, second)]
    load_taps_b.wait()
    block(second, taps_b, scale_b, offset_b, pre_b, act_b, shifts[1])
    wait_all(left + [leave(3, pre_b), leave(4, act_b)])


def ahead(routes, field, slots, first, second, shifts, rows):
    (taps, scale_a, offset_a, point), (taps_b, scale_b, offset_b, _) = first, second
    channels, width = taps.shape[1:]
    units = routes.units
    shape = jax.ShapeDtypeStruct
    thin, wide = (rows, width), (rows, channels)
    return pl.pallas_call(
        functools.partial(ahead_kernel, routes, shifts),
        out_shape=(
            shape(thin, jnp.float32),
            shape(thin, jnp.bfloat16),
            shape(wide, jnp.bfloat16),
            shape(thin, jnp.float32),
            shape(thin, jnp.bfloat16),
        ),
        in_specs=[ANYWHERE] * (1 + len(slots) + 3) + [IN_VMEM] * 4,
        out_specs=[ANYWHERE] * 5,
        scratch_shapes=[
            pltpu.VMEM(wide, jnp.bfloat16),
            pltpu.VMEM(taps.shape, jnp.bfloat16),
            pltpu.VMEM(point.shape, jnp.bfloat16),
            pltpu.VMEM(taps.shape, jnp.bfloat16),
            pltpu.VMEM(thin, jnp.float32),
            pltpu.VMEM(thin, jnp.bfloat16),
            pltpu.VMEM(wide, jnp.bfloat16),
            pltpu.VMEM(thin, jnp.float32),
            pltpu.VMEM(thin, jnp.bfloat16),
            pltpu.SemaphoreType.DMA((units + 8,)),
        ],
        compiler_params=pltpu.CompilerParams(vmem_limit_bytes=VMEM_BYTES),
        cost_estimate=pl.CostEstimate(
            flops=2 * width * channels * 5 * rows,
            bytes_accessed=10 * 2**20,
            transcendentals=2 * rows * width,
        ),
    )(field, *slots, taps, point, taps_b, scale_a, offset_a, scale_b, offset_b)


def split_norms(norms):
    high = norms.astype(jnp.bfloat16)
    low = (norms - high.astype(jnp.float32)).astype(jnp.bfloat16)
    blank = jnp.zeros((NORM_ROWS - 2 * norms.shape[0], norms.shape[1]), jnp.bfloat16)
    return jnp.concatenate([high, low, blank], 0)


def join_norms(rows, count):
    rows = rows.astype(jnp.float32)
    return rows[:count] + rows[count : 2 * count]


def reverse_kernel(routes, count, shifts, *refs):
    steps, units, unit = len(routes.permutes), routes.units, routes.unit
    u_field, u_slots, refs = refs[0], refs[1 : 1 + steps], refs[1 + steps :]
    g_field, g_slots, refs = refs[0], refs[1 : 1 + steps], refs[1 + steps :]
    second_hbm, pre_b_hbm, act_b_hbm, pre_a_hbm, act_a_hbm = refs[:5]
    taps_b_hbm, point_b_hbm, taps_a_hbm, point_a_hbm = refs[5:9]
    scale_a, offset_a, scale_b, offset_b = refs[9:13]
    places = routes.places()
    grad_slots, refs = refs[13 : 13 + len(places)], refs[13 + len(places) :]
    kept_b, sent_b, kept_a, sent_a, norms_ref = refs[:5]
    u_a, g_a, u_b, g_b, pre_a, pre_b, act_a, act_b, taps_a, taps_b, point_a, point_b = refs[5:17]
    grad_act, grad_pre, turned, product, staged, wide, sums, norm_rows, sems, out_sems = refs[17:]
    rows, width = pre_a.shape
    channels = u_a.shape[1]
    share = channels // count
    pad = padded(share)
    half = count // 2 * pad
    seq, chrom = lax.axis_index("seq"), lax.axis_index("chrom")
    core, side, odd, rest = chrom % 2, chrom // 2, seq % 2, seq // 2

    def load(at, source, target):
        return fetch(source, target, sems.at[2 * units + at])

    came_g = fetch_units(routes, g_field, g_slots, g_b, sems, 0)
    loads_b = [load(0, point_b_hbm, point_b), load(1, pre_b_hbm, pre_b)]
    came_second = [load(2, second_hbm, u_b)]
    loads_b += [load(3, act_b_hbm, act_b), load(4, taps_b_hbm, taps_b)]
    loads_a = [load(5, point_a_hbm, point_a), load(6, pre_a_hbm, pre_a)]
    came_u = fetch_units(routes, u_field, u_slots, u_a, sems, units)
    loads_a += [load(7, act_a_hbm, act_a), load(8, taps_a_hbm, taps_a)]

    def block(index, u, g, pre, act, taps, point, loads, came, scale_ref, offset_ref, shift, kept, sent):
        scale, offset = scale_ref[...][None, :], offset_ref[...][None, :]
        loads[0].wait()
        grad_act[...] = across(g[...], point[...])
        sums[...] = jnp.zeros_like(sums)
        steps, step = row_parts(rows)
        loads[1].wait()

        @pl.loop(0, steps, unroll=2 if steps % 2 == 0 else 1)
        def _(at):
            part = pl.ds(pl.multiple_of(at * step, step), step)
            value = pre[part, :]
            normed = scale * value + offset
            grad_norm = grad_act[part, :] * smooth_slope(normed)
            grad_pre[part, :] = (grad_norm * scale).astype(jnp.bfloat16)
            sums[0] += jnp.sum((grad_norm * value).reshape(step // 8, 8, width), 0)
            sums[1] += jnp.sum(grad_norm.reshape(step // 8, 8, width), 0)

        norms = jnp.sum(sums[...], 1)
        norms_ref[2 * index : 2 * index + 2, :] = norms
        norm_rows[index] = split_norms(norms)
        tail = fetch(norm_rows.at[index], sent.at[pl.ds(4 * half, NORM_ROWS)], out_sems.at[index, 8])

        def copies(kind, target):
            source = staged.at[4 * index + kind]
            slot = (kind % 2) ^ side
            for part in range(2):
                place = (slot * 2 + part if index == 1 else part * 2 + slot) * half
                yield pltpu.make_async_copy(
                    source.at[pl.ds(part * half, half)],
                    target.at[pl.ds(pl.multiple_of(place, half), half)],
                    out_sems.at[index, 2 * kind + part],
                )

        def both(kind, act_on):
            @pl.when(core == kind // 2)
            def _():
                for copy in copies(kind, kept):
                    act_on(copy)

            @pl.when(core != kind // 2)
            def _():
                for copy in copies(kind, sent):
                    act_on(copy)

        def settle_one(kind, value):
            if pad != share:
                product[:channels, :] = value
            for at in range(count):
                piece = (value if pad == share else product)[at * share : at * share + pad, :]
                place = ((at % 2) ^ odd) * half + ((at // 2) ^ rest) * pad
                staged[4 * index + kind, pl.ds(pl.multiple_of(place, pad), pad), :] = piece.astype(
                    jnp.bfloat16
                )
            both(kind, lambda copy: copy.start())

        wait_all(came)
        if shift % 128 == 0 and rows % 128 == 0:
            for first in range(0, rows, 128):
                turned[:, first : first + 128] = u[first : first + 128, :].T
            settle_one(0, dot(turned[:, : rows - shift], grad_pre[shift:, :]))
            settle_one(1, dot(turned[...], grad_pre[...]))
            settle_one(2, dot(turned[:, shift:], grad_pre[:-shift, :]))
        else:
            settle_one(0, over_rows(u[:-shift, :], grad_pre[shift:, :]))
            settle_one(1, over_rows(u[...], grad_pre[...]))
            settle_one(2, over_rows(u[shift:, :], grad_pre[:-shift, :]))
        loads[2].wait()
        settle_one(3, over_rows(g[...], act[...]))
        loads[3].wait()
        wide[...] = across(grad_pre[...], taps[1])
        wide[:-shift, :] += across(grad_pre[shift:, :], taps[0])
        wide[shift:, :] += across(grad_pre[:-shift, :], taps[2])
        g_a[...] = (wide[...] + g[...].astype(jnp.float32)).astype(jnp.bfloat16)

        def finish():
            tail.wait()
            for kind in range(4):
                both(kind, lambda copy: copy.wait())

        return finish

    wait_all(came_g)
    finish_b = block(
        1, u_b, g_b, pre_b, act_b, taps_b, point_b, loads_b, came_second, scale_b, offset_b, shifts[1], kept_b, sent_b
    )
    finish_a = block(
        0, u_a, g_a, pre_a, act_a, taps_a, point_a, loads_a, came_u, scale_a, offset_a, shifts[0], kept_a, sent_a
    )
    grads = [
        fetch(unit_at(g_a, pick(places[j], seq), unit), slot, sems.at[j])
        for j, slot in enumerate(grad_slots)
    ]
    finish_b()
    finish_a()
    wait_all(grads)


def reverse(routes, u_field, u_slots, g_field, g_slots, saved, first, second, shifts, rows):
    (taps_a, scale_a, offset_a, point_a), (taps_b, scale_b, offset_b, point_b) = first, second
    pre_a, act_a, second_inputs, pre_b, act_b = saved
    channels, width = taps_a.shape[1:]
    units, count = routes.units, lax.axis_size("seq")
    went = len(routes.places())
    shape = jax.ShapeDtypeStruct
    thin, wide = (rows, width), (rows, channels)
    pad = padded(channels // count)
    kept = shape((2 * count * pad, width), jnp.bfloat16)
    sent = shape((2 * count * pad + NORM_ROWS, width), jnp.bfloat16)
    vmem = pltpu.VMEM
    outs = pl.pallas_call(
        functools.partial(reverse_kernel, routes, count, shifts),
        out_shape=(
            *[shape((routes.unit, channels), jnp.bfloat16)] * went,
            kept,
            sent,
            kept,
            sent,
            shape((4, width), jnp.float32),
        ),
        in_specs=[ANYWHERE] * (2 + len(u_slots) + len(g_slots) + 9) + [IN_VMEM] * 4,
        out_specs=[ANYWHERE] * (went + 4) + [IN_VMEM],
        scratch_shapes=[
            *[vmem(wide, jnp.bfloat16)] * 4,
            *[vmem(thin, jnp.float32)] * 2,
            *[vmem(thin, jnp.bfloat16)] * 2,
            *[vmem(taps_a.shape, jnp.bfloat16)] * 2,
            *[vmem(point_a.shape, jnp.bfloat16)] * 2,
            vmem(thin, jnp.float32),
            vmem(thin, jnp.bfloat16),
            vmem((channels, rows), jnp.bfloat16),
            vmem((8 if pad == channels // count else channels + pad, width), jnp.float32),
            vmem((8, count * pad, width), jnp.bfloat16),
            vmem(wide, jnp.float32),
            vmem((2, 8, width), jnp.float32),
            vmem((2, NORM_ROWS, width), jnp.bfloat16),
            pltpu.SemaphoreType.DMA((2 * units + 9,)),
            pltpu.SemaphoreType.DMA((2, 9)),
        ],
        compiler_params=pltpu.CompilerParams(vmem_limit_bytes=VMEM_BYTES),
        cost_estimate=pl.CostEstimate(
            flops=2 * width * channels * 11 * rows,
            bytes_accessed=18 * 2**20,
            transcendentals=2 * rows * width,
        ),
    )(
        u_field, *u_slots, g_field, *g_slots, second_inputs, pre_b, act_b, pre_a, act_a,
        taps_b, point_b, taps_a, point_a,
        scale_a, offset_a, scale_b, offset_b,
    )
    return outs[:went], outs[went : went + 4], outs[went + 4]


def gather_kernel(routes, *refs):
    parts, out = refs[:-1], refs[-1]
    mine, unit = lax.axis_index("seq"), routes.unit
    for slots, part in zip(routes.slots(), parts):
        out[pl.ds(pl.multiple_of(pick(slots, mine) * unit, unit), unit), :] = part[...]


def gather_units(routes, parts):
    unit, channels = parts[0].shape
    return pl.pallas_call(
        functools.partial(gather_kernel, routes),
        out_shape=jax.ShapeDtypeStruct((routes.units * unit, channels), jnp.bfloat16),
        in_specs=[IN_VMEM] * len(parts),
        out_specs=IN_VMEM,
        cost_estimate=pl.CostEstimate(flops=0, bytes_accessed=2**21, transcendentals=0),
    )(*parts)


def trade(value, axis, bits):
    return lax.ppermute(value, axis, [(i, i ^ bits) for i in range(lax.axis_size(axis))])


def rows_at(block, index, width):
    return pl.BlockSpec((block, width), lambda step: (index, 0))


def summed(parts):
    total = parts[0][...].astype(jnp.float32)
    for part in parts[1:]:
        total = total + part[...].astype(jnp.float32)
    return total


def combine_kernel(number, norms_in, *refs):
    outs = refs[2 * number + 2 : 2 * number + 4]
    norms_out = refs[2 * number + 4]
    for block in range(2):
        parts = refs[block * (number + 1) : (block + 1) * (number + 1)]
        size = parts[0].shape[0]
        norms = norms_in[2 * block : 2 * block + 2, :] + join_norms(parts[number][...], 2)
        norms_out[2 * block : 2 * block + 2, :] = norms
        outs[block][:size, :] = summed(parts[:number]).astype(jnp.bfloat16)
        outs[block][size:, :] = split_norms(norms)


def combine(norms, parts_a, parts_b, waited, vmem_bytes):
    number, width = len(parts_a), norms.shape[1]
    size = (parts_a[-1].shape[0] - NORM_ROWS) // 2
    specs = [rows_at(size, 1, width)] * number + [rows_at(NORM_ROWS, 2 * size // NORM_ROWS, width)]
    shape = jax.ShapeDtypeStruct
    payload = shape((size + NORM_ROWS, width), jnp.bfloat16)
    whole = pl.BlockSpec(payload.shape, lambda step: (0, 0))
    small = pl.BlockSpec(norms.shape, lambda step: (0, 0))

    def kernel(*refs):
        combine_kernel(number, refs[0], *refs[1 : 2 * number + 3], *refs[2 * number + 3 + len(waited) :])

    return pl.pallas_call(
        kernel,
        grid=(1,),
        out_shape=(payload, payload, shape(norms.shape, jnp.float32)),
        in_specs=[small] + specs * 2 + [ANYWHERE] * len(waited),
        out_specs=(whole, whole, small),
        compiler_params=pltpu.CompilerParams(vmem_limit_bytes=vmem_bytes),
        cost_estimate=pl.CostEstimate(flops=0, bytes_accessed=8 * size * width * number, transcendentals=0),
    )(norms, *parts_a, parts_a[-1], *parts_b, parts_b[-1], *waited)


def fold_kernel(kept_a, came_a, kept_b, came_b, out_a, out_b):
    out_a[...] = summed([kept_a, came_a]).astype(jnp.bfloat16)
    out_b[...] = summed([kept_b, came_b]).astype(jnp.bfloat16)


def fold(parts_a, parts_b):
    rows, width = parts_a[0].shape
    half = jax.ShapeDtypeStruct((rows // 2, width), jnp.bfloat16)
    spec = rows_at(rows // 2, 0, width)
    return pl.pallas_call(
        fold_kernel,
        grid=(1,),
        out_shape=(half, half),
        in_specs=[spec] * 4,
        out_specs=(spec, spec),
        compiler_params=pltpu.CompilerParams(vmem_limit_bytes=LATER_VMEM_BYTES),
        cost_estimate=pl.CostEstimate(flops=0, bytes_accessed=6 * rows * width, transcendentals=0),
    )(*parts_a, *parts_b)


def pieces_kernel(number, norms_in, *refs):
    parts, refs = refs[: 2 * number + 2], refs[2 * number + 2 :]
    mine, norms_out, payloads, total = refs[0], refs[1], refs[2:-1], refs[-1]
    pad = mine.shape[0] // 2
    norms = []
    for block in range(2):
        own = parts[block * (number + 1) : (block + 1) * (number + 1)]
        norms.append(norms_in[2 * block : 2 * block + 2, :] + join_norms(own[number][...], 2))
        total[...] = summed(own[:number])
        mine[block * pad : (block + 1) * pad, :] = total[:pad, :]
        for at, payload in enumerate(payloads, 1):
            payload[block * pad : (block + 1) * pad, :] = total[
                at * pad : (at + 1) * pad, :
            ].astype(jnp.bfloat16)
    norms = jnp.concatenate(norms, 0)
    norms_out[...] = norms
    for payload in payloads:
        payload[2 * pad :, :] = split_norms(norms)


def cut_pieces(norms, parts_a, parts_b, share):
    number, width = len(parts_a), norms.shape[1]
    size = parts_a[-1].shape[0] - NORM_ROWS
    pad = padded(share)
    shape = jax.ShapeDtypeStruct
    specs = [rows_at(size, 0, width)] * number + [rows_at(NORM_ROWS, size // NORM_ROWS, width)]
    outs = (
        shape((2 * pad, width), jnp.float32),
        shape(norms.shape, jnp.float32),
        *[shape((2 * pad + NORM_ROWS, width), jnp.bfloat16)] * (size // pad - 1),
    )
    return pl.pallas_call(
        functools.partial(pieces_kernel, number),
        grid=(1,),
        out_shape=outs,
        in_specs=[pl.BlockSpec(norms.shape, lambda step: (0, 0))] + specs * 2,
        out_specs=[pl.BlockSpec(out.shape, lambda step: (0, 0)) for out in outs],
        scratch_shapes=[pltpu.VMEM((size, width), jnp.float32)],
        compiler_params=pltpu.CompilerParams(vmem_limit_bytes=LATER_VMEM_BYTES),
        cost_estimate=pl.CostEstimate(flops=0, bytes_accessed=8 * size * width * number, transcendentals=0),
    )(norms, *parts_a, parts_a[-1], *parts_b, parts_b[-1])


def total_kernel(norms_in, mine, *refs):
    came, out, norms_out = refs[:-2], refs[-2], refs[-1]
    rows = mine.shape[0]
    total, norms = mine[...], norms_in[...]
    for payload in came:
        total = total + payload[:rows, :].astype(jnp.float32)
        norms = norms + join_norms(payload[rows:, :], norms.shape[0])
    out[...] = total.astype(jnp.bfloat16)
    norms_out[...] = norms


def add_pieces(norms, mine, came):
    return pl.pallas_call(
        total_kernel,
        out_shape=(
            jax.ShapeDtypeStruct(mine.shape, jnp.bfloat16),
            jax.ShapeDtypeStruct(norms.shape, jnp.float32),
        ),
        in_specs=[IN_VMEM] * (2 + len(came)),
        out_specs=[IN_VMEM] * 2,
        compiler_params=pltpu.CompilerParams(vmem_limit_bytes=LATER_VMEM_BYTES),
        cost_estimate=pl.CostEstimate(flops=0, bytes_accessed=2**20, transcendentals=0),
    )(norms, mine, *came)


def finish_kernel(factor, share, norms_in, *refs):
    pieces, outs, norms_out = refs[:4], refs[4:8], refs[8:]
    chrom = lax.axis_index("chrom")
    mine = chrom % 2 * 2 + chrom // 2
    for row, out in enumerate(norms_out):
        out[...] = norms_in[row, :] * factor
    pad = pieces[0].shape[0] // 2
    for block in range(2):
        taps, point = outs[2 * block : 2 * block + 2]
        for bits in range(4):
            kind = mine ^ bits
            value = pieces[bits][block * pad : block * pad + share, :].astype(jnp.float32) * factor

            @pl.when(kind < 3)
            def _():
                taps[jnp.minimum(kind, 2)] = value

            @pl.when(kind == 3)
            def _():
                point[...] = value


def finish(norms, pieces, share, factor):
    width = norms.shape[1]
    shape = jax.ShapeDtypeStruct
    pair = [shape((3, share, width), jnp.float32), shape((share, width), jnp.float32)]
    return pl.pallas_call(
        functools.partial(finish_kernel, factor, share),
        out_shape=(*pair, *pair, *[shape((width,), jnp.float32)] * 4),
        in_specs=[IN_VMEM] * 5,
        out_specs=[IN_VMEM] * 8,
        cost_estimate=pl.CostEstimate(flops=0, bytes_accessed=2 * 2**20, transcendentals=0),
    )(norms, *pieces)


def settle(halves, norms, waited, share, factor):
    kept_b, sent_b, kept_a, sent_a = halves
    parts_b, parts_a = [kept_b, trade(sent_b, "chrom", 1)], [kept_a, trade(sent_a, "chrom", 1)]
    sent_a, sent_b, norms = combine(norms, parts_a, parts_b, waited[3:], VMEM_BYTES)
    came_b, came_a = trade(sent_b, "chrom", 2), trade(sent_a, "seq", 1)
    rest_a, rest_b = fold(parts_a, parts_b)
    parts_a, parts_b = [rest_a, came_a], [rest_b, came_b]
    sent_a, sent_b, norms = combine(norms, parts_a, parts_b, waited[:3], LATER_VMEM_BYTES)
    parts_b.append(trade(sent_b, "seq", 1))
    parts_a.append(trade(sent_a, "chrom", 2))
    mine, norms, *payloads = cut_pieces(norms, parts_a, parts_b, share)
    came = [trade(payload, "seq", 2 * b) for b, payload in enumerate(payloads, 1)]
    mine, norms = add_pieces(norms, mine, came)
    side = trade(mine, "chrom", 2)
    pieces = [mine, side, trade(mine, "chrom", 1), trade(side, "chrom", 1)]
    return finish(norms, pieces, share, factor)


def body(
    features,
    first_dilated_taps,
    first_norm_scale,
    first_norm_offset,
    first_pointwise_weight,
    second_dilated_taps,
    second_norm_scale,
    second_norm_offset,
    second_pointwise_weight,
    cotangent,
):
    count = lax.axis_size("seq")
    rows = features.shape[1]
    factor = 1.0 / math.sqrt(rows * count * lax.axis_size("chrom"))
    shifts = DILATION_FIRST // count, DILATION_SECOND // count
    routes = Routes(rows, count)
    first = first_dilated_taps, first_norm_scale, first_norm_offset, first_pointwise_weight
    second = second_dilated_taps, second_norm_scale, second_norm_offset, second_pointwise_weight
    u_slots = routes.out(features[0])
    g_slots = routes.out(cotangent[0])
    saved = ahead(routes, features[0], u_slots, first, second, shifts, rows)
    grads, halves, norms = reverse(
        routes, features[0], u_slots, cotangent[0], g_slots, saved, first, second, shifts, rows
    )
    came = routes.back(grads)
    share = features.shape[2] // count
    conv_a, point_a, conv_b, point_b, *norms = settle(halves, norms, came, share, factor)
    grad_input = gather_units(routes, came + list(grads[len(came) :]))[None]
    return (
        grad_input,
        conv_a, point_a.T, norms[0], norms[1],
        conv_b, point_b.T, norms[2], norms[3],
    )


def solution(mesh):
    in_specs = (
        P("chrom", "seq", None),
        P(),
        P(),
        P(),
        P(),
        P(),
        P(),
        P(),
        P(),
        P("chrom", "seq", None),
    )
    out_specs = (
        P("chrom", "seq", None),
        P(None, "seq", None),
        P(None, "seq"),
        P(),
        P(),
        P(None, "seq", None),
        P(None, "seq"),
        P(),
        P(),
    )
    return jax.shard_map(body, mesh=mesh, in_specs=in_specs, out_specs=out_specs, check_vma=False)
```

```python
import functools
import math

import jax
import jax.numpy as jnp
from jax import lax
from jax.experimental import pallas as pl
from jax.experimental.pallas import tpu as pltpu
from jax.sharding import PartitionSpec as P

DILATION_FIRST = 4096
DILATION_SECOND = 2048
NORM_ROWS = 16
VMEM_BYTES = 56 * 2**20
LATER_VMEM_BYTES = 24 * 2**20

IN_VMEM = pl.BlockSpec(memory_space=pltpu.VMEM)
ANYWHERE = pl.BlockSpec(memory_space=pl.ANY)


def smooth_value(normed):
    return normed * jax.nn.sigmoid(1.702 * normed)


def smooth_slope(normed):
    sigmoid_part = jax.nn.sigmoid(1.702 * normed)
    return sigmoid_part * (1.0 + 1.702 * normed * (1.0 - sigmoid_part))


def dot(left, right):
    return jnp.dot(left, right, preferred_element_type=jnp.float32)


def across(left, right):
    return lax.dot_general(left, right, (((1,), (1,)), ((), ())), preferred_element_type=jnp.float32)


def over_rows(left, right):
    return lax.dot_general(left, right, (((0,), (0,)), ((), ())), preferred_element_type=jnp.float32)


def pick(values, index):
    chosen = jnp.int32(int(values[0]))
    for at, value in enumerate(values[1:], 1):
        chosen = jnp.where(index == at, jnp.int32(int(value)), chosen)
    return chosen


class Routes:
    def __init__(self, rows, count):
        self.unit = math.gcd(rows, DILATION_SECOND // count)
        self.units = rows // self.unit
        same = math.gcd(self.units, count)
        permutes = []
        for j in range(self.units):
            permute = {}
            for i in range(count):
                slot = j // same * same + (j + i // (count // same)) % same
                whole = self.units * i + slot
                permute[i] = slot, whole % count, whole // count
            permutes.append(permute)
        stay, moved = self.without_stays(permutes, count)
        self.stay = stay
        self.permutes = permutes if stay is None else moved
        for permute in self.permutes:
            assert len({target for _, target, _ in permute.values()}) == count

    @staticmethod
    def without_stays(permutes, count):
        stay, moved = {}, []
        for permute in permutes:
            rest = {}
            for i, (slot, target, place) in permute.items():
                if target == i and i not in stay:
                    stay[i] = slot, place
                else:
                    rest[i] = slot, target, place
            for other in moved:
                targets = {target for _, target, _ in other.values()}
                if not (other.keys() & rest.keys()) and not any(t in targets for _, t, _ in rest.values()):
                    other.update(rest)
                    break
            else:
                moved.append(rest)
        if len(stay) != count or any(len(permute) != count for permute in moved):
            return None, None
        return stay, moved

    def slots(self):
        count = len(self.permutes[0])
        found = [[permute[i][0] for i in range(count)] for permute in self.permutes]
        return found if self.stay is None else found + [[self.stay[i][0] for i in range(count)]]

    def places(self):
        count = len(self.permutes[0])
        found = []
        for permute in self.permutes:
            by_target = {target: place for _, target, place in permute.values()}
            found.append([by_target[k] for k in range(count)])
        return found if self.stay is None else found + [[self.stay[k][1] for k in range(count)]]

    def out(self, field):
        mine = lax.axis_index("seq")
        came = []
        for permute in self.permutes:
            slots = [permute[i][0] for i in range(len(permute))]
            kinds = sorted(set(slots))
            part = field[kinds[0] * self.unit : (kinds[0] + 1) * self.unit]
            for kind in kinds[1:]:
                other = field[kind * self.unit : (kind + 1) * self.unit]
                part = jnp.where(pick([slot == kind for slot in slots], mine) == 1, other, part)
            came.append(lax.ppermute(part, "seq", [(i, t) for i, (_, t, _) in permute.items()]))
        return came

    def back(self, parts):
        return [
            lax.ppermute(part, "seq", [(t, i) for i, (_, t, _) in permute.items()])
            for part, permute in zip(parts, self.permutes)
        ]


def fetch(source, target, sem):
    copy = pltpu.make_async_copy(source, target, sem)
    copy.start()
    return copy


def unit_at(ref, place, unit):
    return ref.at[pl.ds(pl.multiple_of(place * unit, unit), unit), :]


def fetch_units(routes, field, came, target, sems, first):
    mine = lax.axis_index("seq")
    places, slots, unit = routes.places(), routes.slots(), routes.unit
    copies = []
    for j, place in enumerate(places):
        source = came[j] if j < len(came) else unit_at(field, pick(slots[j], mine), unit)
        copies.append(fetch(source, unit_at(target, pick(place, mine), unit), sems.at[first + j]))
    return copies


def wait_all(copies):
    for copy in copies:
        copy.wait()


def padded(share):
    return -(-share // 16) * 16


def row_parts(rows):
    step = math.gcd(rows, 32)
    return rows // step, step


def ahead_kernel(routes, shifts, *refs):
    steps, units = len(routes.permutes), routes.units
    field, slots, refs = refs[0], refs[1 : 1 + steps], refs[1 + steps :]
    taps_hbm, point_hbm, taps_b_hbm = refs[:3]
    scale_a, offset_a, scale_b, offset_b = refs[3:7]
    outs, refs = refs[7:12], refs[12:]
    inputs, taps, point, taps_b, pre_a, act_a, second, pre_b, act_b, sems = refs
    rows, width = pre_a.shape
    load_taps = fetch(taps_hbm, taps, sems.at[units])
    came = fetch_units(routes, field, slots, inputs, sems, 0)

    def block(field, taps, scale_ref, offset_ref, pre, act, shift):
        pre[...] = dot(field[...], taps[1])
        pre[shift:, :] += dot(field[:-shift, :], taps[0])
        pre[:-shift, :] += dot(field[shift:, :], taps[2])
        scale, offset = scale_ref[...][None, :], offset_ref[...][None, :]
        steps, step = row_parts(rows)

        @pl.loop(0, steps, unroll=2 if steps % 2 == 0 else 1)
        def _(at):
            part = pl.ds(pl.multiple_of(at * step, step), step)
            act[part, :] = smooth_value(scale * pre[part, :] + offset).astype(jnp.bfloat16)

    def leave(index, source):
        return fetch(source, outs[index], sems.at[units + 3 + index])

    wait_all(came)
    load_taps.wait()
    load_point = fetch(point_hbm, point, sems.at[units + 1])
    load_taps_b = fetch(taps_b_hbm, taps_b, sems.at[units + 2])
    block(inputs, taps, scale_a, offset_a, pre_a, act_a, shifts[0])
    left = [leave(0, pre_a), leave(1, act_a)]
    load_point.wait()
    second[...] = (inputs[...].astype(jnp.float32) + dot(act_a[...], point[...])).astype(jnp.bfloat16)
    left += [leave(2, second)]
    load_taps_b.wait()
    block(second, taps_b, scale_b, offset_b, pre_b, act_b, shifts[1])
    wait_all(left + [leave(3, pre_b), leave(4, act_b)])


def ahead(routes, field, slots, first, second, shifts, rows):
    (taps, scale_a, offset_a, point), (taps_b, scale_b, offset_b, _) = first, second
    channels, width = taps.shape[1:]
    units = routes.units
    shape = jax.ShapeDtypeStruct
    thin, wide = (rows, width), (rows, channels)
    return pl.pallas_call(
        functools.partial(ahead_kernel, routes, shifts),
        out_shape=(
            shape(thin, jnp.float32),
            shape(thin, jnp.bfloat16),
            shape(wide, jnp.bfloat16),
            shape(thin, jnp.float32),
            shape(thin, jnp.bfloat16),
        ),
        in_specs=[ANYWHERE] * (1 + len(slots) + 3) + [IN_VMEM] * 4,
        out_specs=[ANYWHERE] * 5,
        scratch_shapes=[
            pltpu.VMEM(wide, jnp.bfloat16),
            pltpu.VMEM(taps.shape, jnp.bfloat16),
            pltpu.VMEM(point.shape, jnp.bfloat16),
            pltpu.VMEM(taps.shape, jnp.bfloat16),
            pltpu.VMEM(thin, jnp.float32),
            pltpu.VMEM(thin, jnp.bfloat16),
            pltpu.VMEM(wide, jnp.bfloat16),
            pltpu.VMEM(thin, jnp.float32),
            pltpu.VMEM(thin, jnp.bfloat16),
            pltpu.SemaphoreType.DMA((units + 8,)),
        ],
        compiler_params=pltpu.CompilerParams(vmem_limit_bytes=VMEM_BYTES),
        cost_estimate=pl.CostEstimate(
            flops=2 * width * channels * 5 * rows,
            bytes_accessed=10 * 2**20,
            transcendentals=2 * rows * width,
        ),
    )(field, *slots, taps, point, taps_b, scale_a, offset_a, scale_b, offset_b)


def split_norms(norms):
    high = norms.astype(jnp.bfloat16)
    low = (norms - high.astype(jnp.float32)).astype(jnp.bfloat16)
    blank = jnp.zeros((NORM_ROWS - 2 * norms.shape[0], norms.shape[1]), jnp.bfloat16)
    return jnp.concatenate([high, low, blank], 0)


def join_norms(rows, count):
    rows = rows.astype(jnp.float32)
    return rows[:count] + rows[count : 2 * count]


def reverse_kernel(routes, count, shifts, *refs):
    steps, units, unit = len(routes.permutes), routes.units, routes.unit
    u_field, u_slots, refs = refs[0], refs[1 : 1 + steps], refs[1 + steps :]
    g_field, g_slots, refs = refs[0], refs[1 : 1 + steps], refs[1 + steps :]
    second_hbm, pre_b_hbm, act_b_hbm, pre_a_hbm, act_a_hbm = refs[:5]
    taps_b_hbm, point_b_hbm, taps_a_hbm, point_a_hbm = refs[5:9]
    scale_a, offset_a, scale_b, offset_b = refs[9:13]
    places = routes.places()
    grad_slots, refs = refs[13 : 13 + len(places)], refs[13 + len(places) :]
    kept_b, sent_b, kept_a, sent_a, norms_ref = refs[:5]
    u_a, g_a, u_b, g_b, pre_a, pre_b, act_a, act_b, taps_a, taps_b, point_a, point_b = refs[5:17]
    grad_act, grad_pre, turned, product, staged, wide, sums, norm_rows, sems, out_sems = refs[17:]
    rows, width = pre_a.shape
    channels = u_a.shape[1]
    share = channels // count
    pad = padded(share)
    half = count // 2 * pad
    seq, chrom = lax.axis_index("seq"), lax.axis_index("chrom")
    core, side, odd, rest = chrom % 2, chrom // 2, seq % 2, seq // 2

    def load(at, source, target):
        return fetch(source, target, sems.at[2 * units + at])

    came_g = fetch_units(routes, g_field, g_slots, g_b, sems, 0)
    loads_b = [load(0, point_b_hbm, point_b), load(1, pre_b_hbm, pre_b)]
    came_second, loads_a, came_u = [], [], []

    def load_rest_b():
        came_second.append(load(2, second_hbm, u_b))
        loads_b.extend([load(3, act_b_hbm, act_b), load(4, taps_b_hbm, taps_b)])

    def load_a():
        loads_a.extend([load(5, point_a_hbm, point_a), load(6, pre_a_hbm, pre_a)])
        came_u.extend(fetch_units(routes, u_field, u_slots, u_a, sems, units))
        loads_a.extend([load(7, act_a_hbm, act_a), load(8, taps_a_hbm, taps_a)])

    def block(index, u, g, pre, act, taps, point, loads, came, scale_ref, offset_ref, shift, kept, sent):
        scale, offset = scale_ref[...][None, :], offset_ref[...][None, :]
        loads[0].wait()
        if index == 1:
            load_rest_b()
        grad_act[...] = across(g[...], point[...])
        sums[...] = jnp.zeros_like(sums)
        steps, step = row_parts(rows)
        loads[1].wait()

        @pl.loop(0, steps, unroll=2 if steps % 2 == 0 else 1)
        def _(at):
            part = pl.ds(pl.multiple_of(at * step, step), step)
            value = pre[part, :]
            normed = scale * value + offset
            grad_norm = grad_act[part, :] * smooth_slope(normed)
            grad_pre[part, :] = (grad_norm * scale).astype(jnp.bfloat16)
            sums[0] += jnp.sum((grad_norm * value).reshape(step // 8, 8, width), 0)
            sums[1] += jnp.sum(grad_norm.reshape(step // 8, 8, width), 0)

        if index == 1:
            load_a()
        norms = jnp.sum(sums[...], 1)
        norms_ref[2 * index : 2 * index + 2, :] = norms
        norm_rows[index] = split_norms(norms)
        tail = fetch(norm_rows.at[index], sent.at[pl.ds(4 * half, NORM_ROWS)], out_sems.at[index, 8])

        def copies(kind, target):
            source = staged.at[4 * index + kind]
            slot = (kind % 2) ^ side
            for part in range(2):
                place = (slot * 2 + part if index == 1 else part * 2 + slot) * half
                yield pltpu.make_async_copy(
                    source.at[pl.ds(part * half, half)],
                    target.at[pl.ds(pl.multiple_of(place, half), half)],
                    out_sems.at[index, 2 * kind + part],
                )

        def both(kind, act_on):
            @pl.when(core == kind // 2)
            def _():
                for copy in copies(kind, kept):
                    act_on(copy)

            @pl.when(core != kind // 2)
            def _():
                for copy in copies(kind, sent):
                    act_on(copy)

        def settle_one(kind, value):
            if pad != share:
                product[:channels, :] = value
            for at in range(count):
                piece = (value if pad == share else product)[at * share : at * share + pad, :]
                place = ((at % 2) ^ odd) * half + ((at // 2) ^ rest) * pad
                staged[4 * index + kind, pl.ds(pl.multiple_of(place, pad), pad), :] = piece.astype(
                    jnp.bfloat16
                )
            both(kind, lambda copy: copy.start())

        wait_all(came)
        if shift % 128 == 0 and rows % 128 == 0:
            for first in range(0, rows, 128):
                turned[:, first : first + 128] = u[first : first + 128, :].T
            settle_one(0, dot(turned[:, : rows - shift], grad_pre[shift:, :]))
            settle_one(1, dot(turned[...], grad_pre[...]))
            settle_one(2, dot(turned[:, shift:], grad_pre[:-shift, :]))
        else:
            settle_one(0, over_rows(u[:-shift, :], grad_pre[shift:, :]))
            settle_one(1, over_rows(u[...], grad_pre[...]))
            settle_one(2, over_rows(u[shift:, :], grad_pre[:-shift, :]))
        loads[2].wait()
        settle_one(3, over_rows(g[...], act[...]))
        loads[3].wait()
        wide[...] = across(grad_pre[...], taps[1])
        wide[:-shift, :] += across(grad_pre[shift:, :], taps[0])
        wide[shift:, :] += across(grad_pre[:-shift, :], taps[2])
        g_a[...] = (wide[...] + g[...].astype(jnp.float32)).astype(jnp.bfloat16)

        def finish():
            tail.wait()
            for kind in range(4):
                both(kind, lambda copy: copy.wait())

        return finish

    wait_all(came_g)
    finish_b = block(
        1, u_b, g_b, pre_b, act_b, taps_b, point_b, loads_b, came_second, scale_b, offset_b, shifts[1], kept_b, sent_b
    )
    finish_a = block(
        0, u_a, g_a, pre_a, act_a, taps_a, point_a, loads_a, came_u, scale_a, offset_a, shifts[0], kept_a, sent_a
    )
    grads = [
        fetch(unit_at(g_a, pick(places[j], seq), unit), slot, sems.at[j])
        for j, slot in enumerate(grad_slots)
    ]
    finish_b()
    finish_a()
    wait_all(grads)


def reverse(routes, u_field, u_slots, g_field, g_slots, saved, first, second, shifts, rows):
    (taps_a, scale_a, offset_a, point_a), (taps_b, scale_b, offset_b, point_b) = first, second
    pre_a, act_a, second_inputs, pre_b, act_b = saved
    channels, width = taps_a.shape[1:]
    units, count = routes.units, lax.axis_size("seq")
    went = len(routes.places())
    shape = jax.ShapeDtypeStruct
    thin, wide = (rows, width), (rows, channels)
    pad = padded(channels // count)
    kept = shape((2 * count * pad, width), jnp.bfloat16)
    sent = shape((2 * count * pad + NORM_ROWS, width), jnp.bfloat16)
    vmem = pltpu.VMEM
    outs = pl.pallas_call(
        functools.partial(reverse_kernel, routes, count, shifts),
        out_shape=(
            *[shape((routes.unit, channels), jnp.bfloat16)] * went,
            kept,
            sent,
            kept,
            sent,
            shape((4, width), jnp.float32),
        ),
        in_specs=[ANYWHERE] * (2 + len(u_slots) + len(g_slots) + 9) + [IN_VMEM] * 4,
        out_specs=[ANYWHERE] * (went + 4) + [IN_VMEM],
        scratch_shapes=[
            *[vmem(wide, jnp.bfloat16)] * 4,
            *[vmem(thin, jnp.float32)] * 2,
            *[vmem(thin, jnp.bfloat16)] * 2,
            *[vmem(taps_a.shape, jnp.bfloat16)] * 2,
            *[vmem(point_a.shape, jnp.bfloat16)] * 2,
            vmem(thin, jnp.float32),
            vmem(thin, jnp.bfloat16),
            vmem((channels, rows), jnp.bfloat16),
            vmem((8 if pad == channels // count else channels + pad, width), jnp.float32),
            vmem((8, count * pad, width), jnp.bfloat16),
            vmem(wide, jnp.float32),
            vmem((2, 8, width), jnp.float32),
            vmem((2, NORM_ROWS, width), jnp.bfloat16),
            pltpu.SemaphoreType.DMA((2 * units + 9,)),
            pltpu.SemaphoreType.DMA((2, 9)),
        ],
        compiler_params=pltpu.CompilerParams(vmem_limit_bytes=VMEM_BYTES),
        cost_estimate=pl.CostEstimate(
            flops=2 * width * channels * 11 * rows,
            bytes_accessed=18 * 2**20,
            transcendentals=2 * rows * width,
        ),
    )(
        u_field, *u_slots, g_field, *g_slots, second_inputs, pre_b, act_b, pre_a, act_a,
        taps_b, point_b, taps_a, point_a,
        scale_a, offset_a, scale_b, offset_b,
    )
    return outs[:went], outs[went : went + 4], outs[went + 4]


def gather_kernel(routes, *refs):
    parts, out = refs[:-1], refs[-1]
    mine, unit = lax.axis_index("seq"), routes.unit
    for slots, part in zip(routes.slots(), parts):
        out[pl.ds(pl.multiple_of(pick(slots, mine) * unit, unit), unit), :] = part[...]


def gather_units(routes, parts):
    unit, channels = parts[0].shape
    return pl.pallas_call(
        functools.partial(gather_kernel, routes),
        out_shape=jax.ShapeDtypeStruct((routes.units * unit, channels), jnp.bfloat16),
        in_specs=[IN_VMEM] * len(parts),
        out_specs=IN_VMEM,
        cost_estimate=pl.CostEstimate(flops=0, bytes_accessed=2**21, transcendentals=0),
    )(*parts)


def trade(value, axis, bits):
    return lax.ppermute(value, axis, [(i, i ^ bits) for i in range(lax.axis_size(axis))])


def rows_at(block, index, width):
    return pl.BlockSpec((block, width), lambda step: (index, 0))


def summed(parts):
    total = parts[0][...].astype(jnp.float32)
    for part in parts[1:]:
        total = total + part[...].astype(jnp.float32)
    return total


def combine_kernel(number, norms_in, *refs):
    outs = refs[2 * number + 2 : 2 * number + 4]
    norms_out = refs[2 * number + 4]
    for block in range(2):
        parts = refs[block * (number + 1) : (block + 1) * (number + 1)]
        size = parts[0].shape[0]
        norms = norms_in[2 * block : 2 * block + 2, :] + join_norms(parts[number][...], 2)
        norms_out[2 * block : 2 * block + 2, :] = norms
        outs[block][:size, :] = summed(parts[:number]).astype(jnp.bfloat16)
        outs[block][size:, :] = split_norms(norms)


def combine(norms, parts_a, parts_b, waited, vmem_bytes):
    number, width = len(parts_a), norms.shape[1]
    size = (parts_a[-1].shape[0] - NORM_ROWS) // 2
    specs = [rows_at(size, 1, width)] * number + [rows_at(NORM_ROWS, 2 * size // NORM_ROWS, width)]
    shape = jax.ShapeDtypeStruct
    payload = shape((size + NORM_ROWS, width), jnp.bfloat16)
    whole = pl.BlockSpec(payload.shape, lambda step: (0, 0))
    small = pl.BlockSpec(norms.shape, lambda step: (0, 0))

    def kernel(*refs):
        combine_kernel(number, refs[0], *refs[1 : 2 * number + 3], *refs[2 * number + 3 + len(waited) :])

    return pl.pallas_call(
        kernel,
        grid=(1,),
        out_shape=(payload, payload, shape(norms.shape, jnp.float32)),
        in_specs=[small] + specs * 2 + [ANYWHERE] * len(waited),
        out_specs=(whole, whole, small),
        compiler_params=pltpu.CompilerParams(vmem_limit_bytes=vmem_bytes),
        cost_estimate=pl.CostEstimate(flops=0, bytes_accessed=8 * size * width * number, transcendentals=0),
    )(norms, *parts_a, parts_a[-1], *parts_b, parts_b[-1], *waited)


def fold_kernel(kept_a, came_a, kept_b, came_b, out_a, out_b):
    out_a[...] = summed([kept_a, came_a]).astype(jnp.bfloat16)
    out_b[...] = summed([kept_b, came_b]).astype(jnp.bfloat16)


def fold(parts_a, parts_b):
    rows, width = parts_a[0].shape
    half = jax.ShapeDtypeStruct((rows // 2, width), jnp.bfloat16)
    spec = rows_at(rows // 2, 0, width)
    return pl.pallas_call(
        fold_kernel,
        grid=(1,),
        out_shape=(half, half),
        in_specs=[spec] * 4,
        out_specs=(spec, spec),
        compiler_params=pltpu.CompilerParams(vmem_limit_bytes=LATER_VMEM_BYTES),
        cost_estimate=pl.CostEstimate(flops=0, bytes_accessed=6 * rows * width, transcendentals=0),
    )(*parts_a, *parts_b)


def pieces_kernel(number, norms_in, *refs):
    parts, refs = refs[: 2 * number + 2], refs[2 * number + 2 :]
    mine, norms_out, payloads, total = refs[0], refs[1], refs[2:-1], refs[-1]
    pad = mine.shape[0] // 2
    norms = []
    for block in range(2):
        own = parts[block * (number + 1) : (block + 1) * (number + 1)]
        norms.append(norms_in[2 * block : 2 * block + 2, :] + join_norms(own[number][...], 2))
        total[...] = summed(own[:number])
        mine[block * pad : (block + 1) * pad, :] = total[:pad, :]
        for at, payload in enumerate(payloads, 1):
            payload[block * pad : (block + 1) * pad, :] = total[
                at * pad : (at + 1) * pad, :
            ].astype(jnp.bfloat16)
    norms = jnp.concatenate(norms, 0)
    norms_out[...] = norms
    for payload in payloads:
        payload[2 * pad :, :] = split_norms(norms)


def cut_pieces(norms, parts_a, parts_b, share):
    number, width = len(parts_a), norms.shape[1]
    size = parts_a[-1].shape[0] - NORM_ROWS
    pad = padded(share)
    shape = jax.ShapeDtypeStruct
    specs = [rows_at(size, 0, width)] * number + [rows_at(NORM_ROWS, size // NORM_ROWS, width)]
    outs = (
        shape((2 * pad, width), jnp.float32),
        shape(norms.shape, jnp.float32),
        *[shape((2 * pad + NORM_ROWS, width), jnp.bfloat16)] * (size // pad - 1),
    )
    return pl.pallas_call(
        functools.partial(pieces_kernel, number),
        grid=(1,),
        out_shape=outs,
        in_specs=[pl.BlockSpec(norms.shape, lambda step: (0, 0))] + specs * 2,
        out_specs=[pl.BlockSpec(out.shape, lambda step: (0, 0)) for out in outs],
        scratch_shapes=[pltpu.VMEM((size, width), jnp.float32)],
        compiler_params=pltpu.CompilerParams(vmem_limit_bytes=LATER_VMEM_BYTES),
        cost_estimate=pl.CostEstimate(flops=0, bytes_accessed=8 * size * width * number, transcendentals=0),
    )(norms, *parts_a, parts_a[-1], *parts_b, parts_b[-1])


def total_kernel(norms_in, mine, *refs):
    came, out, norms_out = refs[:-2], refs[-2], refs[-1]
    rows = mine.shape[0]
    total, norms = mine[...], norms_in[...]
    for payload in came:
        total = total + payload[:rows, :].astype(jnp.float32)
        norms = norms + join_norms(payload[rows:, :], norms.shape[0])
    out[...] = total.astype(jnp.bfloat16)
    norms_out[...] = norms


def add_pieces(norms, mine, came):
    return pl.pallas_call(
        total_kernel,
        out_shape=(
            jax.ShapeDtypeStruct(mine.shape, jnp.bfloat16),
            jax.ShapeDtypeStruct(norms.shape, jnp.float32),
        ),
        in_specs=[IN_VMEM] * (2 + len(came)),
        out_specs=[IN_VMEM] * 2,
        compiler_params=pltpu.CompilerParams(vmem_limit_bytes=LATER_VMEM_BYTES),
        cost_estimate=pl.CostEstimate(flops=0, bytes_accessed=2**20, transcendentals=0),
    )(norms, mine, *came)


def finish_kernel(factor, share, norms_in, *refs):
    pieces, outs, norms_out = refs[:4], refs[4:8], refs[8:]
    chrom = lax.axis_index("chrom")
    mine = chrom % 2 * 2 + chrom // 2
    for row, out in enumerate(norms_out):
        out[...] = norms_in[row, :] * factor
    pad = pieces[0].shape[0] // 2
    for block in range(2):
        taps, point = outs[2 * block : 2 * block + 2]
        for bits in range(4):
            kind = mine ^ bits
            value = pieces[bits][block * pad : block * pad + share, :].astype(jnp.float32) * factor

            @pl.when(kind < 3)
            def _():
                taps[jnp.minimum(kind, 2)] = value

            @pl.when(kind == 3)
            def _():
                point[...] = value


def finish(norms, pieces, share, factor):
    width = norms.shape[1]
    shape = jax.ShapeDtypeStruct
    pair = [shape((3, share, width), jnp.float32), shape((share, width), jnp.float32)]
    return pl.pallas_call(
        functools.partial(finish_kernel, factor, share),
        out_shape=(*pair, *pair, *[shape((width,), jnp.float32)] * 4),
        in_specs=[IN_VMEM] * 5,
        out_specs=[IN_VMEM] * 8,
        cost_estimate=pl.CostEstimate(flops=0, bytes_accessed=2 * 2**20, transcendentals=0),
    )(norms, *pieces)


def settle(halves, norms, waited, share, factor):
    kept_b, sent_b, kept_a, sent_a = halves
    parts_b, parts_a = [kept_b, trade(sent_b, "chrom", 1)], [kept_a, trade(sent_a, "chrom", 1)]
    sent_a, sent_b, norms = combine(norms, parts_a, parts_b, waited[3:], VMEM_BYTES)
    came_b, came_a = trade(sent_b, "chrom", 2), trade(sent_a, "seq", 1)
    rest_a, rest_b = fold(parts_a, parts_b)
    parts_a, parts_b = [rest_a, came_a], [rest_b, came_b]
    sent_a, sent_b, norms = combine(norms, parts_a, parts_b, waited[:3], LATER_VMEM_BYTES)
    parts_b.append(trade(sent_b, "seq", 1))
    parts_a.append(trade(sent_a, "chrom", 2))
    mine, norms, *payloads = cut_pieces(norms, parts_a, parts_b, share)
    came = [trade(payload, "seq", 2 * b) for b, payload in enumerate(payloads, 1)]
    mine, norms = add_pieces(norms, mine, came)
    side = trade(mine, "chrom", 2)
    pieces = [mine, side, trade(mine, "chrom", 1), trade(side, "chrom", 1)]
    return finish(norms, pieces, share, factor)


def body(
    features,
    first_dilated_taps,
    first_norm_scale,
    first_norm_offset,
    first_pointwise_weight,
    second_dilated_taps,
    second_norm_scale,
    second_norm_offset,
    second_pointwise_weight,
    cotangent,
):
    count = lax.axis_size("seq")
    rows = features.shape[1]
    factor = 1.0 / math.sqrt(rows * count * lax.axis_size("chrom"))
    shifts = DILATION_FIRST // count, DILATION_SECOND // count
    routes = Routes(rows, count)
    first = first_dilated_taps, first_norm_scale, first_norm_offset, first_pointwise_weight
    second = second_dilated_taps, second_norm_scale, second_norm_offset, second_pointwise_weight
    u_slots = routes.out(features[0])
    g_slots = routes.out(cotangent[0])
    saved = ahead(routes, features[0], u_slots, first, second, shifts, rows)
    grads, halves, norms = reverse(
        routes, features[0], u_slots, cotangent[0], g_slots, saved, first, second, shifts, rows
    )
    came = routes.back(grads)
    share = features.shape[2] // count
    conv_a, point_a, conv_b, point_b, *norms = settle(halves, norms, came, share, factor)
    grad_input = gather_units(routes, came + list(grads[len(came) :]))[None]
    return (
        grad_input,
        conv_a, point_a.T, norms[0], norms[1],
        conv_b, point_b.T, norms[2], norms[3],
    )


def solution(mesh):
    in_specs = (
        P("chrom", "seq", None),
        P(),
        P(),
        P(),
        P(),
        P(),
        P(),
        P(),
        P(),
        P("chrom", "seq", None),
    )
    out_specs = (
        P("chrom", "seq", None),
        P(None, "seq", None),
        P(None, "seq"),
        P(),
        P(),
        P(None, "seq", None),
        P(None, "seq"),
        P(),
        P(),
    )
    return jax.shard_map(body, mesh=mesh, in_specs=in_specs, out_specs=out_specs, check_vma=False)
```
